256 devices in a mesh: dp: 32 (over z, y), ctx: 8 (over x, core).
Axes of the slice: x: 4, y: 4, z: 8, core: 2. Of those that a mesh axis runs over, the one named last changes fastest.
Arguments:
- uvqk: bfloat16 [32, 1024, 4096], P(None, 'ctx', 'dp'), may hold values from -1.5 to 1.5
- lengths: int32 [32], replicated, may hold values from 1 to 1024, as said below
- assignment: int32 [32], replicated, may hold values from 0 to 31, as said below
- buckets: int32 [1024], replicated, may hold values from 0 to 127
- rel_bias: float32 [8, 128], replicated, may hold values from -3 to 3
- cotangent: bfloat16 [32, 1024, 1024], P('dp', 'ctx'), may hold values from -6 to 6
Outputs:
- output: bfloat16 [32, 1024, 1024], P('dp', 'ctx')
- d_uvqk: bfloat16 [32, 1024, 4096], P(None, 'ctx', 'dp')
- d_bias: float32 [8, 128], replicated
The draws below stay inside these ranges and needn't reach their ends.
Inputs may be any that keep to these rules, and one draw needn't show every extreme that they name: `lengths`: valid actions of each user; some user has exactly 1024. `assignment`: A permutation of the user ids. Slot d * 1 + t is the t-th slot of index d of dp; users are dealt to slots in order of falling length, alternating the direction over dp from one round to the next (with 1 = 1 there is a single round: slot d holds the user of rank d).
All inputs are finite; a program needn't handle non-finite values.
Results may differ from the reference program's by a relative error of at most 0.0055.
Values may be sent and summed in bfloat16 or wider, within the bound.
A program may use at most 128 MiB of HBM per device.

```python
import jax
import jax.numpy as jnp
from jax import lax

D = 1024
H = 8
NB = 128
LEN = 1024
U_DEV = 1
USERS = 32


def user_lengths(key):
    first, second, third = jax.random.split(key, 3)
    shifts = jax.random.randint(first, (USERS,), 0, 4)
    base_len = jnp.right_shift(jnp.int32(LEN), shifts.astype(jnp.int32))
    reduction = jax.random.randint(second, (USERS,), 0, LEN) % jnp.maximum(base_len // 2, 1)
    result = base_len - reduction
    longest = jax.random.randint(third, (), 0, USERS)
    result = jnp.where(jnp.arange(USERS, dtype=jnp.int32) == longest, LEN, result)
    return result.astype(jnp.int32)


def draw_lengths(key, part):
    return user_lengths(key)


def draw_assignment(key, part):
    sizes_drawn = user_lengths(key)
    key = jax.random.fold_in(key, 7)
    tiebreak = jax.random.permutation(key, USERS).astype(jnp.int32)
    ranking = jnp.argsort(-(sizes_drawn * USERS + tiebreak), stable=True).astype(jnp.int32)
    device_count = USERS // U_DEV
    ranks = jnp.arange(USERS, dtype=jnp.int32)
    rounds = ranks // device_count
    places = ranks % device_count
    device = jnp.where(rounds % 2 == 0, places, device_count - 1 - places)
    target = device * U_DEV + rounds
    return jnp.zeros((USERS,), jnp.int32).at[target].set(ranking)


def place_ends(values, key, smallest, high):
    longest = values.shape.index(max(values.shape))
    spots = []
    for shift in (0, 1):
        where = [jax.random.randint(jax.random.fold_in(key, axis), (), 0, length) for axis, length in enumerate(values.shape)]
        where[longest] = (where[longest] + shift) % values.shape[longest]
        spots.append(tuple(where))
    return values.at[spots[0]].set(smallest).at[spots[1]].set(high)


def block_scale(key, dims, cuts, smallest, largest):
    level = 1.0
    for dim, shards_of in cuts:
        draws = jax.random.uniform(jax.random.fold_in(jax.random.fold_in(key, 6), dim), (shards_of,), jnp.float32, smallest / len(cuts), largest / len(cuts))
        level = level * jnp.repeat(jnp.exp(draws), dims[dim] // shards_of).reshape((-1,) + (1,) * (len(dims) - 1 - dim))
    return level


def gaussian(own_key, shape, spread, limit, cuts=(), kind=jnp.bfloat16):
    level = block_scale(own_key, shape, cuts, -0.22, 0.18) if cuts else 1.0
    entries = jax.random.normal(own_key, shape, jnp.float32) * spread * level
    return jnp.minimum(jnp.maximum(entries, -limit), limit).astype(kind)


def setup_inputs(seed: int = 0) -> dict:
    streams_of = jax.random.split(jax.random.key(seed), 7)
    uvqk = gaussian(streams_of[0], (USERS, LEN, 4 * D), 0.3, 1.5, ((1, 8), (2, 32)))
    lengths = draw_lengths(jax.random.fold_in(streams_of[6], 71), 0)
    assignment = draw_assignment(jax.random.fold_in(streams_of[6], 71), 0)
    buckets = place_ends(jax.random.randint(streams_of[3], (LEN,), 0, NB), jax.random.fold_in(streams_of[3], 1), 0, NB - 1).astype(jnp.int32)
    rel_bias = gaussian(streams_of[4], (H, NB), 0.5, 3.0, (), jnp.float32)
    cotangent = gaussian(streams_of[5], (USERS, LEN, D), 1.0, 6.0, ((0, 32), (1, 8)))
    return {"uvqk": uvqk, "lengths": lengths, "assignment": assignment, "buckets": buckets, "rel_bias": rel_bias, "cotangent": cotangent}


def split_heads(matrix):
    return matrix.reshape(matrix.shape[0], H, D // H)

def reference(uvqk, lengths, assignment, buckets, rel_bias, cotangent):
    span_rows = min(256, LEN)
    block_count = LEN // span_rows
    relative = rel_bias[:, buckets]
    positions = jnp.arange(LEN, dtype=jnp.int32)
    highest = lax.Precision.HIGHEST
    head_dim = D // H

    def one_user(slot):
        user = assignment[slot]
        inputs = uvqk[user].astype(jnp.float32)
        valid_len = lengths[user]
        upstream = cotangent[slot].astype(jnp.float32)
        gate_up = inputs[:, :D]
        values = split_heads(inputs[:, D:2 * D])
        queries = split_heads(inputs[:, 2 * D:3 * D])
        keys_all = split_heads(inputs[:, 3 * D:])

        def pair_terms(q_index, k_index):
            q_lo = q_index * span_rows
            k_lo = k_index * span_rows
            q_pos = positions[q_lo:q_lo + span_rows]
            k_pos = positions[k_lo:k_lo + span_rows]
            distance = q_pos[:, None] - k_pos[None, :]
            nearest = jnp.clip(distance, 0, LEN - 1)
            score = jnp.einsum('ihd,jhd->hij', queries[q_lo:q_lo + span_rows], keys_all[k_lo:k_lo + span_rows], precision=highest) + relative[:, nearest]
            live = (distance >= 0) & (q_pos < valid_len)[:, None] & (k_pos < valid_len)[None, :]
            weight = jnp.where(live[None], jax.nn.silu(score), 0.0).astype(jnp.bfloat16)
            weight = lax.optimization_barrier(weight).astype(jnp.float32)
            return (score, live, nearest, weight)

        def empty_block():
            return jnp.zeros((span_rows, H, head_dim), jnp.float32)
        attended = []
        for q_index in range(block_count):
            total_sum = empty_block()
            for k_index in range(q_index + 1):

                def contribute(q_index=q_index, k_index=k_index):
                    score, live, nearest, weight = pair_terms(q_index, k_index)
                    k_lo = k_index * span_rows
                    return jnp.einsum('hij,jhd->ihd', weight, values[k_lo:k_lo + span_rows], precision=highest)
                total_sum = total_sum + lax.cond(k_index * span_rows < valid_len, contribute, empty_block)
            attended.append(total_sum)
        attended = jnp.concatenate(attended, 0).reshape(LEN, D)
        mean = attended.mean(-1, keepdims=True)
        centered = attended - mean
        variance = (centered * centered).mean(-1, keepdims=True)
        inverse_std = lax.rsqrt(variance + 1e-05)
        normed = centered * inverse_std
        output = (normed * gate_up).astype(jnp.bfloat16)
        grad_norm = upstream * gate_up
        d_up = (upstream * normed).astype(jnp.bfloat16)
        d_attended = (grad_norm - grad_norm.mean(-1, keepdims=True) - normed * (grad_norm * normed).mean(-1, keepdims=True)) * inverse_std
        d_attended = lax.optimization_barrier(d_attended.astype(jnp.bfloat16)).astype(jnp.float32)
        d_heads = split_heads(d_attended)
        d_query = [empty_block() for index in range(block_count)]
        d_key = [empty_block() for index in range(block_count)]
        d_value = [empty_block() for index in range(block_count)]
        d_bias = jnp.zeros((H, NB), jnp.float32)

        def empty_grads():
            return (empty_block(), empty_block(), empty_block(), jnp.zeros((H, NB), jnp.float32))
        for q_index in range(block_count):
            for k_index in range(q_index + 1):

                def gradient(q_index=q_index, k_index=k_index):
                    score, live, nearest, weight = pair_terms(q_index, k_index)
                    q_lo = q_index * span_rows
                    k_lo = k_index * span_rows
                    d_weight = jnp.einsum('ihd,jhd->hij', d_heads[q_lo:q_lo + span_rows], values[k_lo:k_lo + span_rows], precision=highest)
                    sigma = jax.nn.sigmoid(score)
                    d_score = jnp.where(live[None], d_weight * sigma * (1.0 + score * (1.0 - sigma)), 0.0)
                    d_score_b = lax.optimization_barrier(d_score.astype(jnp.bfloat16)).astype(jnp.float32)
                    part_q = jnp.einsum('hij,jhd->ihd', d_score_b, keys_all[k_lo:k_lo + span_rows], precision=highest)
                    part_k = jnp.einsum('hij,ihd->jhd', d_score_b, queries[q_lo:q_lo + span_rows], precision=highest)
                    part_v = jnp.einsum('hij,ihd->jhd', weight, d_heads[q_lo:q_lo + span_rows], precision=highest)
                    pair_bucket = buckets[nearest].reshape(-1)
                    part_b = jax.vmap(lambda plane: jax.ops.segment_sum(plane.reshape(-1), pair_bucket, num_segments=NB))(d_score)
                    return (part_q, part_k, part_v, part_b)
                part_q, part_k, part_v, part_b = lax.cond(k_index * span_rows < valid_len, gradient, empty_grads)
                d_query[q_index] = d_query[q_index] + part_q
                d_key[k_index] = d_key[k_index] + part_k
                d_value[k_index] = d_value[k_index] + part_v
                d_bias = d_bias + part_b
        d_query = jnp.concatenate(d_query, 0).reshape(LEN, D).astype(jnp.bfloat16)
        d_key = jnp.concatenate(d_key, 0).reshape(LEN, D).astype(jnp.bfloat16)
        d_value = jnp.concatenate(d_value, 0).reshape(LEN, D).astype(jnp.bfloat16)
        grads = jnp.concatenate([d_up, d_value, d_query, d_key], -1)
        return (output, grads, d_bias)
    outputs, grads, biases = lax.map(one_user, jnp.arange(USERS, dtype=jnp.int32))
    d_uvqk = jnp.zeros_like(grads).at[assignment].set(grads)
    return (outputs, d_uvqk, biases.sum(0))
```

```python
import functools

import jax
import jax.numpy as jnp
from jax import lax
from jax.experimental import pallas as pl
from jax.experimental.pallas import tpu as pltpu
from jax.sharding import PartitionSpec as P

MESH = pl.DeviceIdType.MESH
TB = 256
W = 128
NN = (((1,), (0,)), ((), ()))
NT = (((1,), (1,)), ((), ()))


def mm(a, b, dims):
    return lax.dot_general(a, b, dims, preferred_element_type=jnp.float32)


def tile_at(ib, jb):
    return ib * (ib + 1) // 2 + jb


def kernel(
    H,
    U,
    assign,
    inverse,
    lengths,
    uvqk,
    cot,
    buckets,
    rel,
    out,
    grads,
    dbias,
    in_send,
    in_recv,
    cot_recv,
    out_send,
    g_send,
    g_recv,
    toep,
    wts,
    dsl,
    diag,
    vt,
    kt,
    ut,
    gt,
    at,
    dat,
    st_recv,
    st_send,
    db_send,
    db_recv,
    db_sum,
    db_all,
    s_in,
    r_in,
    s_cot,
    r_cot,
    s_st,
    r_st,
    s_out,
    r_out,
    s_g,
    r_g,
    s_db,
    r_db,
    s_dba,
    r_dba,
):
    k = lax.axis_index("dp")
    c = lax.axis_index("ctx")
    e = lax.rem(k, H)
    comp = lax.div(k, H)
    own = jnp.logical_and(e == c, True)
    LEN = H * W
    nt = LEN // TB
    per = TB // W

    def remote(src, dst, ss, rs, dev):
        return pltpu.make_async_remote_copy(
            src_ref=src, dst_ref=dst, send_sem=ss, recv_sem=rs, device_id=dev, device_id_type=MESH
        )

    barrier = pltpu.get_barrier_semaphore()

    def greet_slots(o, _):
        d = lax.rem(k + o, U)

        @pl.when(jnp.logical_not(jnp.logical_and(o == 0, own)))
        def _():
            pl.semaphore_signal(barrier, inc=1, device_id=(d, e), device_id_type=MESH)

        return 0

    lax.fori_loop(0, U, greet_slots, 0)

    def greet_owners(o, _):
        kk = lax.div(o, H) * H + c
        cc = lax.rem(o, H)

        @pl.when(jnp.logical_not(jnp.logical_and(kk == k, cc == c)))
        def _():
            pl.semaphore_signal(barrier, inc=1, device_id=(kk, cc), device_id_type=MESH)

        return 0

    lax.fori_loop(0, 4 * H, greet_owners, 0)

    def greet_ctx(o, _):
        pl.semaphore_signal(
            barrier, inc=1, device_id=(k, lax.rem(c + o, H)), device_id_type=MESH
        )
        return 0

    lax.fori_loop(1, H, greet_ctx, 0)

    def arrange(d, _):
        in_send[d] = uvqk[assign[d]]
        return 0

    lax.fori_loop(0, U, arrange, 0)

    pl.semaphore_wait(barrier, U + 4 * H + H - 1 - 2 * own.astype(jnp.int32))

    def in_copy(o):
        d = lax.rem(k + o, U)
        return remote(
            in_send.at[d],
            in_recv.at[comp, pl.ds(pl.multiple_of(c * W, W), W)],
            s_in.at[o],
            r_in.at[comp * H + c],
            (d, e),
        )

    def in_start(o, _):
        in_copy(o).start()
        return 0

    @pl.when(jnp.logical_not(own))
    def _():
        in_copy(0).start()

    @pl.when(own)
    def _():
        pltpu.make_async_copy(
            in_send.at[k],
            in_recv.at[comp, pl.ds(pl.multiple_of(c * W, W), W)],
            r_in.at[comp * H + c],
        ).start()

    lax.fori_loop(1, U, in_start, 0)

    def cot_copy(o):
        cc = lax.rem(c + o, H)
        return remote(
            cot.at[:, pl.ds(pl.multiple_of(cc * W, W), W)],
            cot_recv.at[pl.ds(pl.multiple_of(c * W, W), W)],
            s_cot.at[o],
            r_cot.at[c],
            (k, cc),
        )

    def cot_start(o, _):
        cot_copy(o).start()
        return 0

    lax.fori_loop(1, H, cot_start, 0)
    cot_recv[pl.ds(pl.multiple_of(c * W, W), W), :] = cot[:, pl.ds(pl.multiple_of(c * W, W), W)]

    eye = lax.broadcasted_iota(jnp.int32, (W, W), 0) == lax.broadcasted_iota(
        jnp.int32, (W, W), 1
    )
    onehot = lax.broadcasted_iota(jnp.int32, (W, LEN), 0) == buckets[...]
    rel_col = jnp.sum(jnp.where(eye, rel[pl.ds(c, 1), :], 0.0), axis=1, keepdims=True)
    relative = jnp.sum(jnp.where(onehot, rel_col, 0.0), axis=0, keepdims=True)
    row8 = lax.broadcasted_iota(jnp.int32, (8, 2 * TB), 0)
    for m in range(nt):
        low = relative[:, m * TB : (m + 1) * TB]
        before = relative[:, (m - 1) * TB : m * TB] if m else low
        x = jnp.broadcast_to(jnp.concatenate([low, before], 1), (8, 2 * TB))
        for bit in (1, 2, 4):
            x = jnp.where((row8 & bit) != 0, pltpu.roll(x, bit, 1), x)
        size = 8
        while size < TB:
            x = jnp.concatenate([x, pltpu.roll(x, size, 1)], 0)
            size *= 2
        toep[m] = x[:, :TB]

    def in_wait(which):
        def step(o, _):
            ref = in_recv.at[which, pl.ds(pl.multiple_of(o * W, W), W)]
            remote(ref, ref, s_in.at[0], r_in.at[which * H + o], (k, c)).wait_recv()
            return 0

        lax.fori_loop(0, H, step, 0)

    user_len = lengths[assign[k]]

    for which in (1, 2, 3):
        in_wait(which)
    for r in range(H):
        vt[:, r * W : (r + 1) * W] = (
            in_recv[1, r * W : (r + 1) * W].astype(jnp.float32).T.astype(jnp.bfloat16)
        )

    key_at = lax.broadcasted_iota(jnp.int32, (TB, TB), 0)
    for ib in range(nt):
        query_at = lax.broadcasted_iota(jnp.int32, (1, TB), 1) + ib * TB
        limit = jnp.where(query_at < user_len, query_at, -1)
        q = in_recv[2, ib * TB : (ib + 1) * TB]
        acc = jnp.zeros((W, TB), jnp.float32)
        for jb in range(ib + 1):
            t = tile_at(ib, jb)
            score = mm(in_recv[3, jb * TB : (jb + 1) * TB], q, NT) + toep[ib - jb]
            live = key_at <= limit - jb * TB
            sig = 0.5 + 0.5 * jnp.tanh(0.5 * score)
            weight = score * sig
            slope = sig + weight * (1.0 - sig)
            wb = jnp.where(live, weight, 0.0).astype(jnp.bfloat16)
            wts[t] = wb
            dsl[t] = jnp.where(live, slope, 0.0)
            acc = acc + mm(vt[:, jb * TB : (jb + 1) * TB], wb, NN)
        at[:, ib * TB : (ib + 1) * TB] = acc

    in_wait(0)

    def cot_wait(o, _):
        cc = lax.rem(c + o, H)
        ref = cot_recv.at[pl.ds(pl.multiple_of(cc * W, W), W)]
        remote(ref, ref, s_cot.at[0], r_cot.at[cc], (k, cc)).wait_recv()
        return 0

    lax.fori_loop(1, H, cot_wait, 0)

    means, spreads, gsums, gdots = [], [], [], []
    for r in range(H):
        rows = slice(r * W, (r + 1) * W)
        up = in_recv[0, rows].astype(jnp.float32).T
        grad = cot_recv[rows].astype(jnp.float32).T * up
        ut[:, rows] = up
        gt[:, rows] = grad
        a = at[:, rows]
        mean = jnp.sum(a, axis=0, keepdims=True) * (1.0 / W)
        centered = a - mean
        means.append(mean)
        spreads.append(jnp.sum(centered * centered, axis=0, keepdims=True))
        gsums.append(jnp.sum(grad, axis=0, keepdims=True))
        gdots.append(jnp.sum(grad * centered, axis=0, keepdims=True))
    for n, rows_of in enumerate((means, spreads, gsums, gdots)):
        st_send[n] = jnp.concatenate(rows_of, 0)

    def st_copy(o):
        cc = lax.rem(c + o, H)
        return remote(st_send, st_recv.at[c], s_st.at[o], r_st.at[c], (k, cc))

    def st_start(o, _):
        st_copy(o).start()
        return 0

    lax.fori_loop(1, H, st_start, 0)
    st_recv[c] = st_send[...]
    for r in range(H):
        kt[:, r * W : (r + 1) * W] = (
            in_recv[3, r * W : (r + 1) * W].astype(jnp.float32).T.astype(jnp.bfloat16)
        )

    def st_wait(o, _):
        cc = lax.rem(c + o, H)
        ref = st_recv.at[cc]
        remote(ref, ref, s_st.at[0], r_st.at[cc], (k, cc)).wait_recv()
        return 0

    lax.fori_loop(1, H, st_wait, 0)

    D = H * W
    mean = st_recv[0, 0]
    for h in range(1, H):
        mean = mean + st_recv[h, 0]
    mean = mean * (1.0 / H)
    square = jnp.zeros_like(mean)
    g_total = jnp.zeros_like(mean)
    gn_total = jnp.zeros_like(mean)
    for h in range(H):
        off = st_recv[h, 0] - mean
        square = square + (st_recv[h, 1] + W * (off * off))
        g_total = g_total + st_recv[h, 2]
        gn_total = gn_total + (st_recv[h, 3] + off * st_recv[h, 2])
    inv = lax.rsqrt(square * (1.0 / D) + 1e-05)
    g_mean = g_total * (1.0 / D)
    gn_mean = gn_total * inv * (1.0 / D)
    for r in range(H):
        rows = slice(r * W, (r + 1) * W)
        row = slice(r, r + 1)
        normed = (at[:, rows] - mean[row]) * inv[row]
        dat[:, rows] = (
            (gt[:, rows] - g_mean[row] - normed * gn_mean[row]) * inv[row]
        ).astype(jnp.bfloat16)
        natural = normed.T
        up = in_recv[0, rows].astype(jnp.float32)
        out_send[rows] = (natural * up).astype(jnp.bfloat16)
        g_send[0, rows] = (natural * cot_recv[rows].astype(jnp.float32)).astype(jnp.bfloat16)

    def g_copy(which, o):
        cc = lax.rem(c + o, H)
        return remote(
            g_send.at[which, pl.ds(pl.multiple_of(cc * W, W), W)],
            g_recv.at[k],
            s_g.at[which * H + o],
            r_g.at[k],
            (which * H + c, cc),
        )

    def g_start(which):
        mine = which * H + c == k

        @pl.when(jnp.logical_not(mine))
        def _():
            g_copy(which, 0).start()

        @pl.when(mine)
        def _():
            pltpu.make_async_copy(
                g_send.at[which, pl.ds(pl.multiple_of(c * W, W), W)], g_recv.at[k], r_g.at[k]
            ).start()

        def step(o, _):
            g_copy(which, o).start()
            return 0

        lax.fori_loop(1, H, step, 0)

    def out_copy(o):
        cc = lax.rem(c + o, H)
        return remote(
            out_send.at[pl.ds(pl.multiple_of(cc * W, W), W)],
            out.at[:, pl.ds(pl.multiple_of(c * W, W), W)],
            s_out.at[o],
            r_out.at[c],
            (k, cc),
        )

    def out_start(o, _):
        out_copy(o).start()
        return 0

    g_start(0)
    lax.fori_loop(1, H, out_start, 0)
    out[:, pl.ds(pl.multiple_of(c * W, W), W)] = out_send[pl.ds(pl.multiple_of(c * W, W), W), :]

    for jb in range(nt):
        acc = jnp.zeros((TB, W), jnp.float32)
        for ib in range(jb, nt):
            acc = acc + mm(wts[tile_at(ib, jb)], dat[:, ib * TB : (ib + 1) * TB], NT)
        g_send[1, jb * TB : (jb + 1) * TB] = acc.astype(jnp.bfloat16)
    g_start(1)

    q_acc = [jnp.zeros((W, TB), jnp.float32) for _ in range(nt)]
    for jb in range(nt):
        value = in_recv[1, jb * TB : (jb + 1) * TB]
        acc = jnp.zeros((TB, W), jnp.float32)
        for ib in range(jb, nt):
            t = tile_at(ib, jb)
            ds = mm(value, dat[:, ib * TB : (ib + 1) * TB], NN) * dsl[t]
            if jb == 0:
                diag[ib - jb] = ds
            else:
                diag[ib - jb] += ds
            dsb = ds.astype(jnp.bfloat16)
            acc = acc + mm(dsb, in_recv[2, ib * TB : (ib + 1) * TB], NN)
            q_acc[ib] = q_acc[ib] + mm(kt[:, jb * TB : (jb + 1) * TB], dsb, NN)
        g_send[3, jb * TB : (jb + 1) * TB] = acc.astype(jnp.bfloat16)
    g_start(3)
    for ib in range(nt):
        for p in range(per):
            r = ib * per + p
            g_send[2, r * W : (r + 1) * W] = (
                q_acc[ib][:, p * W : (p + 1) * W].T.astype(jnp.bfloat16)
            )
    g_start(2)

    sheared = []
    for m in range(nt):
        x = jnp.concatenate([diag[m], jnp.zeros((TB, TB), jnp.float32)], 1)
        size = TB
        while size > 8:
            size //= 2
            x = x[:size] + pltpu.roll(x[size:], 2 * TB - size, 1)
        for bit in (1, 2, 4):
            x = jnp.where((row8 & bit) != 0, pltpu.roll(x, 2 * TB - bit, 1), x)
        sheared.append(jnp.sum(x, axis=0, keepdims=True))
    by_distance = []
    for m in range(nt):
        part = sheared[m][:, :TB]
        if m + 1 < nt:
            part = part + sheared[m + 1][:, TB:]
        by_distance.append(part)
    by_distance = jnp.concatenate(by_distance, 1)
    db_col = jnp.sum(jnp.where(onehot, by_distance, 0.0), axis=1, keepdims=True)
    db_send[0] = jnp.sum(jnp.where(eye, db_col, 0.0), axis=0, keepdims=True)

    def db_dev(o):
        return lax.div(o, H) * H + c, lax.rem(o, H)

    def db_start(o, _):
        kk, cc = db_dev(o)

        @pl.when(jnp.logical_not(jnp.logical_and(kk == k, cc == c)))
        def _():
            remote(db_send.at[0], db_recv.at[k], s_db.at[o], r_db.at[k], (kk, cc)).start()

        return 0

    lax.fori_loop(0, 4 * H, db_start, 0)

    @pl.when(own)
    def _():
        db_recv[k] = db_send[0]

    def db_wait(o, _):
        d = lax.rem(k + o, U)

        @pl.when(jnp.logical_not(jnp.logical_and(o == 0, own)))
        def _():
            ref = db_recv.at[d]
            remote(ref, ref, s_db.at[0], r_db.at[d], (d, e)).wait_recv()

        return 0

    lax.fori_loop(0, U, db_wait, 0)
    db_sum[0] = jnp.sum(db_recv[...], axis=0)

    def dba_start(cc, _):
        kk = comp * H + c

        @pl.when(jnp.logical_not(jnp.logical_and(kk == k, cc == c)))
        def _():
            remote(db_sum.at[0], db_all.at[e], s_dba.at[cc], r_dba.at[e], (kk, cc)).start()

        return 0

    lax.fori_loop(0, H, dba_start, 0)

    @pl.when(own)
    def _():
        db_all[e] = db_sum[0]

    def dba_wait(j, _):
        @pl.when(jnp.logical_not(jnp.logical_and(j == e, own)))
        def _():
            ref = db_all.at[j]
            remote(ref, ref, s_dba.at[0], r_dba.at[j], (comp * H + j, e)).wait_recv()

        return 0

    lax.fori_loop(0, H, dba_wait, 0)
    for j in range(H):
        dbias[j : j + 1, :] = db_all[j]

    def g_wait(d, _):
        ref = g_recv.at[d]
        remote(ref, ref, s_g.at[0], r_g.at[d], (d, e)).wait_recv()
        return 0

    lax.fori_loop(0, U, g_wait, 0)

    def place(u, _):
        grads[u] = g_recv[inverse[u]]
        return 0

    lax.fori_loop(0, U, place, 0)

    def out_wait(o, _):
        cc = lax.rem(c + o, H)
        ref = out.at[:, pl.ds(pl.multiple_of(cc * W, W), W)]
        remote(ref, ref, s_out.at[0], r_out.at[cc], (k, cc)).wait_recv()
        return 0

    lax.fori_loop(1, H, out_wait, 0)

    @pl.when(jnp.logical_not(own))
    def _():
        in_copy(0).wait_send()

    def in_left(o, _):
        in_copy(o).wait_send()
        return 0

    lax.fori_loop(1, U, in_left, 0)

    def ctx_left(o, _):
        cot_copy(o).wait_send()
        st_copy(o).wait_send()
        out_copy(o).wait_send()
        for which in range(4):
            g_copy(which, o).wait_send()
        return 0

    lax.fori_loop(1, H, ctx_left, 0)
    for which in range(4):

        @pl.when(which * H + c != k)
        def _(which=which):
            g_copy(which, 0).wait_send()

    def db_left(o, _):
        kk, cc = db_dev(o)

        @pl.when(jnp.logical_not(jnp.logical_and(kk == k, cc == c)))
        def _():
            remote(db_send.at[0], db_recv.at[k], s_db.at[o], r_db.at[k], (kk, cc)).wait_send()

        return 0

    lax.fori_loop(0, 4 * H, db_left, 0)

    def dba_left(cc, _):
        kk = comp * H + c

        @pl.when(jnp.logical_not(jnp.logical_and(kk == k, cc == c)))
        def _():
            remote(db_sum.at[0], db_all.at[e], s_dba.at[cc], r_dba.at[e], (kk, cc)).wait_send()

        return 0

    lax.fori_loop(0, H, dba_left, 0)


def on_device(uvqk, lengths, assignment, buckets, rel_bias, cotangent):
    U = assignment.shape[0]
    H = rel_bias.shape[0]
    LEN = buckets.shape[0]
    D = H * W
    nt = LEN // TB
    tiles = nt * (nt + 1) // 2
    users = jnp.arange(U, dtype=jnp.int32)
    inverse = jnp.sum(jnp.where(assignment[None, :] == users[:, None], users[None, :], 0), axis=1)
    vm = pl.BlockSpec(memory_space=pltpu.VMEM)
    sm = pl.BlockSpec(memory_space=pltpu.SMEM)
    bf, f32 = jnp.bfloat16, jnp.float32
    dma = pltpu.SemaphoreType.DMA
    out, grads, dbias = pl.pallas_call(
        functools.partial(kernel, H, U),
        out_shape=[
            jax.ShapeDtypeStruct((W, D), bf),
            jax.ShapeDtypeStruct((U, W, W), bf),
            jax.ShapeDtypeStruct((H, W), f32),
        ],
        in_specs=[sm, sm, sm, vm, vm, vm, vm],
        out_specs=[vm, vm, vm],
        scratch_shapes=[
            pltpu.VMEM((U, W, W), bf),
            pltpu.VMEM((4, LEN, W), bf),
            pltpu.VMEM((LEN, W), bf),
            pltpu.VMEM((LEN, W), bf),
            pltpu.VMEM((4, LEN, W), bf),
            pltpu.VMEM((U, W, W), bf),
            pltpu.VMEM((nt, TB, TB), f32),
            pltpu.VMEM((tiles, TB, TB), bf),
            pltpu.VMEM((tiles, TB, TB), f32),
            pltpu.VMEM((nt, TB, TB), f32),
            pltpu.VMEM((W, LEN), bf),
            pltpu.VMEM((W, LEN), bf),
            pltpu.VMEM((W, LEN), f32),
            pltpu.VMEM((W, LEN), f32),
            pltpu.VMEM((W, LEN), f32),
            pltpu.VMEM((W, LEN), bf),
            pltpu.VMEM((H, 4, H, W), f32),
            pltpu.VMEM((4, H, W), f32),
            pltpu.VMEM((1, 1, W), f32),
            pltpu.VMEM((U, 1, W), f32),
            pltpu.VMEM((1, 1, W), f32),
            pltpu.VMEM((H, 1, W), f32),
            dma((U,)),
            dma((4 * H,)),
            dma((H,)),
            dma((H,)),
            dma((H,)),
            dma((H,)),
            dma((H,)),
            dma((H,)),
            dma((4 * H,)),
            dma((U,)),
            dma((4 * H,)),
            dma((U,)),
            dma((H,)),
            dma((H,)),
        ],
        compiler_params=pltpu.CompilerParams(
            collective_id=0, has_side_effects=True, vmem_limit_bytes=40 * 1024 * 1024
        ),
        name="layer",
    )(
        assignment,
        inverse,
        lengths,
        uvqk,
        cotangent.reshape(W, D),
        buckets.reshape(1, LEN),
        rel_bias,
    )
    return out.reshape(1, W, D), grads, dbias


def solution(mesh):
    in_specs = (P(None, "ctx", "dp"), P(), P(), P(), P(), P("dp", "ctx", None))
    out_specs = (P("dp", "ctx", None), P(None, "ctx", "dp"), P())
    return jax.shard_map(
        on_device, mesh=mesh, in_specs=in_specs, out_specs=out_specs, check_vma=False
    )
```

```python
import functools

import jax
import jax.numpy as jnp
from jax import lax
from jax.experimental import pallas as pl
from jax.experimental.pallas import tpu as pltpu
from jax.sharding import PartitionSpec as P

MESH = pl.DeviceIdType.MESH
TB = 256
W = 128
NN = (((1,), (0,)), ((), ()))
NT = (((1,), (1,)), ((), ()))


def mm(a, b, dims):
    return lax.dot_general(a, b, dims, preferred_element_type=jnp.float32)


def tile_at(ib, jb):
    return ib * (ib + 1) // 2 + jb


def ctx_of(h, p, H):
    if H != 8:
        return h
    y, b = lax.rem(h, 4), lax.div(h, 4)
    return lax.rem(y + 2 * b + lax.rem(p, 4), 4) * 2 + b


def head_of(c, p, H):
    if H != 8:
        return c
    x, b = lax.div(c, 2), lax.rem(c, 2)
    return b * 4 + lax.rem(x + 8 - 2 * b - lax.rem(p, 4), 4)


def kernel(
    H,
    U,
    assign_hbm,
    lengths_hbm,
    uvqk_hbm,
    cot_hbm,
    buckets_hbm,
    rel_hbm,
    out,
    grads,
    dbias,
    assign,
    lengths,
    uvqk,
    cot,
    buckets,
    rel,
    in_send,
    in_recv,
    cot_recv,
    out_send,
    g_send,
    toep,
    wts,
    dsl,
    diag,
    vt,
    kt,
    gt,
    at,
    dat,
    st_recv,
    st_send,
    db_send,
    db_recv,
    db_sum,
    db_mine,
    db_all,
    s_load,
    s_in,
    r_in,
    s_cot,
    r_cot,
    s_st,
    r_st,
    s_out,
    r_out,
    s_g,
    r_g,
    s_db,
    r_db,
    s_dbs,
    r_dbs,
    s_dba,
    r_dba,
):
    k = lax.axis_index("dp")
    c = lax.axis_index("ctx")
    e = lax.rem(k, H)
    comp = lax.div(k, H)
    head = head_of(c, k, H)
    own = e == head
    LEN = H * W
    nt = LEN // TB
    per = TB // W

    def rows(cc):
        if isinstance(cc, int):
            return pl.ds(cc * W, W)
        return pl.ds(pl.multiple_of(cc * W, W), W)

    def remote(src, dst, ss, rs, dev):
        return pltpu.make_async_remote_copy(
            src_ref=src, dst_ref=dst, send_sem=ss, recv_sem=rs, device_id=dev, device_id_type=MESH
        )

    def arrived(ref, ss, rs):
        remote(ref, ref, ss, rs, (k, c)).wait_recv()

    def loop(lo, hi, body):
        def step(i, _):
            body(i)
            return 0

        lax.fori_loop(lo, hi, step, 0)

    loads = [
        pltpu.make_async_copy(src, dst, s_load.at[n])
        for n, (src, dst) in enumerate(
            (
                (assign_hbm, assign),
                (uvqk_hbm, uvqk),
                (cot_hbm, cot),
                (lengths_hbm, lengths),
                (buckets_hbm, buckets),
                (rel_hbm, rel),
            )
        )
    ]
    for load in loads:
        load.start()
    barrier = pltpu.get_barrier_semaphore()

    for o in range(4 * H):
        kk, cc = o // H * H + head, o % H

        @pl.when(jnp.logical_not(jnp.logical_and(kk == k, cc == c)))
        def _(kk=kk, cc=cc):
            pl.semaphore_signal(barrier, inc=1, device_id=(kk, cc), device_id_type=MESH)

    for o in range(1, H):
        pl.semaphore_signal(
            barrier, inc=1, device_id=(k, lax.rem(c + o, H)), device_id_type=MESH
        )

    for load in loads:
        load.wait()

    def arrange(p):
        in_send[p] = uvqk[assign[p]]

    loop(0, U, arrange)
    pl.semaphore_wait(barrier, U + H - 1 - own.astype(jnp.int32))

    def in_copy(o):
        p = lax.rem(k + o, U)
        return remote(
            in_send.at[p],
            in_recv.at[comp, rows(c)],
            s_in.at[o],
            r_in.at[comp * H + c],
            (p, ctx_of(e, p, H)),
        )

    @pl.when(jnp.logical_not(own))
    def _():
        in_copy(0).start()

    @pl.when(own)
    def _():
        pltpu.make_async_copy(
            in_send.at[k], in_recv.at[comp, rows(c)], r_in.at[comp * H + c]
        ).start()

    for o in range(1, U):
        in_copy(o).start()

    def cot_copy(o):
        cc = lax.rem(c + o, H)
        return remote(
            cot.at[:, rows(head_of(cc, k, H))],
            cot_recv.at[rows(c)],
            s_cot.at[o],
            r_cot.at[c],
            (k, cc),
        )

    for o in range(1, H):
        cot_copy(o).start()
    cot_recv[rows(c), :] = cot[:, rows(head)]

    eye = lax.broadcasted_iota(jnp.int32, (W, W), 0) == lax.broadcasted_iota(
        jnp.int32, (W, W), 1
    )
    onehot = lax.broadcasted_iota(jnp.int32, (W, LEN), 0) == buckets[...]
    rel_col = jnp.sum(jnp.where(eye, rel[pl.ds(head, 1), :], 0.0), axis=1, keepdims=True)
    relative = jnp.sum(jnp.where(onehot, rel_col, 0.0), axis=0, keepdims=True)
    row8 = lax.broadcasted_iota(jnp.int32, (8, 2 * TB), 0)
    for m in range(nt):
        low = relative[:, m * TB : (m + 1) * TB]
        before = relative[:, (m - 1) * TB : m * TB] if m else low
        x = jnp.broadcast_to(jnp.concatenate([low, before], 1), (8, 2 * TB))
        for bit in (1, 2, 4):
            x = jnp.where((row8 & bit) != 0, pltpu.roll(x, bit, 1), x)
        size = 8
        while size < TB:
            x = jnp.concatenate([x, pltpu.roll(x, size, 1)], 0)
            size *= 2
        toep[m] = x[:, :TB]

    def in_wait(which):
        loop(
            0,
            H,
            lambda cc: arrived(
                in_recv.at[which, rows(cc)], s_in.at[0], r_in.at[which * H + cc]
            ),
        )

    user_len = lengths[assign[k]]
    for which in (1, 2, 3):
        in_wait(which)
    for r in range(H):
        vt[:, r * W : (r + 1) * W] = (
            in_recv[1, r * W : (r + 1) * W].astype(jnp.float32).T.astype(jnp.bfloat16)
        )

    key_at = lax.broadcasted_iota(jnp.int32, (TB, TB), 0)
    for ib in range(nt):
        query_at = lax.broadcasted_iota(jnp.int32, (1, TB), 1) + ib * TB
        limit = jnp.where(query_at < user_len, query_at, -1)
        q = in_recv[2, ib * TB : (ib + 1) * TB]
        acc = jnp.zeros((W, TB), jnp.float32)
        for jb in range(ib + 1):
            t = tile_at(ib, jb)
            score = mm(in_recv[3, jb * TB : (jb + 1) * TB], q, NT) + toep[ib - jb]
            live = key_at <= limit - jb * TB
            sig = 0.5 + 0.5 * jnp.tanh(0.5 * score)
            weight = score * sig
            slope = sig + weight * (1.0 - sig)
            wb = jnp.where(live, weight, 0.0).astype(jnp.bfloat16)
            wts[t] = wb
            dsl[t] = jnp.where(live, slope, 0.0)
            acc = acc + mm(vt[:, jb * TB : (jb + 1) * TB], wb, NN)
        at[:, ib * TB : (ib + 1) * TB] = acc

    in_wait(0)

    def cot_wait(o):
        cc = lax.rem(c + o, H)
        arrived(cot_recv.at[rows(cc)], s_cot.at[0], r_cot.at[cc])

    loop(1, H, cot_wait)

    means, spreads, gsums, gdots = [], [], [], []
    for r in range(H):
        blk = slice(r * W, (r + 1) * W)
        grad = (cot_recv[blk].astype(jnp.float32) * in_recv[0, blk].astype(jnp.float32)).T
        gt[:, blk] = grad
        a = at[:, blk]
        mean = jnp.sum(a, axis=0, keepdims=True) * (1.0 / W)
        centered = a - mean
        means.append(mean)
        spreads.append(jnp.sum(centered * centered, axis=0, keepdims=True))
        gsums.append(jnp.sum(grad, axis=0, keepdims=True))
        gdots.append(jnp.sum(grad * centered, axis=0, keepdims=True))
    for n, rows_of in enumerate((means, spreads, gsums, gdots)):
        st_send[n] = jnp.concatenate(rows_of, 0)

    def st_copy(o):
        cc = lax.rem(c + o, H)
        return remote(st_send, st_recv.at[c], s_st.at[o], r_st.at[c], (k, cc))

    loop(1, H, lambda o: st_copy(o).start())
    st_recv[c] = st_send[...]
    for r in range(H):
        kt[:, r * W : (r + 1) * W] = (
            in_recv[3, r * W : (r + 1) * W].astype(jnp.float32).T.astype(jnp.bfloat16)
        )

    def st_wait(o):
        cc = lax.rem(c + o, H)
        arrived(st_recv.at[cc], s_st.at[0], r_st.at[cc])

    loop(1, H, st_wait)

    D = H * W
    mean = st_recv[0, 0]
    for h in range(1, H):
        mean = mean + st_recv[h, 0]
    mean = mean * (1.0 / H)
    square = jnp.zeros_like(mean)
    g_total = jnp.zeros_like(mean)
    gn_total = jnp.zeros_like(mean)
    for h in range(H):
        off = st_recv[h, 0] - mean
        square = square + (st_recv[h, 1] + W * (off * off))
        g_total = g_total + st_recv[h, 2]
        gn_total = gn_total + (st_recv[h, 3] + off * st_recv[h, 2])
    inv = lax.rsqrt(square * (1.0 / D) + 1e-05)
    g_mean = g_total * (1.0 / D)
    gn_mean = gn_total * inv * (1.0 / D)
    for r in range(H):
        blk = slice(r * W, (r + 1) * W)
        row = slice(r, r + 1)
        normed = (at[:, blk] - mean[row]) * inv[row]
        dat[:, blk] = (
            (gt[:, blk] - g_mean[row] - normed * gn_mean[row]) * inv[row]
        ).astype(jnp.bfloat16)
        natural = normed.T
        out_send[blk] = (natural * in_recv[0, blk].astype(jnp.float32)).astype(jnp.bfloat16)
        g_send[0, blk] = (natural * cot_recv[blk].astype(jnp.float32)).astype(jnp.bfloat16)

    def g_copy(which, o):
        cc = lax.rem(c + o, H)
        return remote(
            g_send.at[which, rows(cc)],
            grads.at[k],
            s_g.at[which * H + o],
            r_g.at[k],
            (which * H + head, cc),
        )

    def g_start(o):
        for n in range(4):
            which = lax.rem(comp + n, 4)
            copy = g_copy(which, o)
            if o > 0:
                copy.start()
                continue
            mine = which * H + head == k

            @pl.when(jnp.logical_not(mine))
            def _(copy=copy):
                copy.start()

            @pl.when(mine)
            def _(which=which):
                pltpu.make_async_copy(g_send.at[which, rows(c)], grads.at[k], r_g.at[k]).start()

    def g_left(o):
        for which in range(4):
            if o > 0:
                g_copy(which, o).wait_send()
                continue

            @pl.when(which * H + head != k)
            def _(which=which):
                g_copy(which, 0).wait_send()

    def out_copy(o):
        cc = lax.rem(c + o, H)
        return remote(
            out_send.at[rows(cc)], out.at[:, rows(head)], s_out.at[o], r_out.at[c], (k, cc)
        )

    for o in range(1, H):
        out_copy(o).start()
    keep = pltpu.make_async_copy(out_send.at[rows(c)], out.at[:, rows(head)], s_out.at[0])
    keep.start()

    q_acc = [jnp.zeros((W, TB), jnp.float32) for _ in range(nt)]
    for jb in range(nt):
        value = in_recv[1, jb * TB : (jb + 1) * TB]
        acc = jnp.zeros((TB, W), jnp.float32)
        for ib in range(jb, nt):
            t = tile_at(ib, jb)
            ds = mm(value, dat[:, ib * TB : (ib + 1) * TB], NN) * dsl[t]
            if jb == 0:
                diag[ib - jb] = ds
            else:
                diag[ib - jb] += ds
            dsb = ds.astype(jnp.bfloat16)
            acc = acc + mm(dsb, in_recv[2, ib * TB : (ib + 1) * TB], NN)
            q_acc[ib] = q_acc[ib] + mm(kt[:, jb * TB : (jb + 1) * TB], dsb, NN)
        g_send[3, jb * TB : (jb + 1) * TB] = acc.astype(jnp.bfloat16)
    sheared = []
    for m in range(nt):
        x = jnp.concatenate([diag[m], jnp.zeros((TB, TB), jnp.float32)], 1)
        size = TB
        while size > 8:
            size //= 2
            x = x[:size] + pltpu.roll(x[size:], 2 * TB - size, 1)
        for bit in (1, 2, 4):
            x = jnp.where((row8 & bit) != 0, pltpu.roll(x, 2 * TB - bit, 1), x)
        sheared.append(jnp.sum(x, axis=0, keepdims=True))
    by_distance = []
    for m in range(nt):
        part = sheared[m][:, :TB]
        if m + 1 < nt:
            part = part + sheared[m + 1][:, TB:]
        by_distance.append(part)
    by_distance = jnp.concatenate(by_distance, 1)
    db_col = jnp.sum(jnp.where(onehot, by_distance, 0.0), axis=1, keepdims=True)
    db_send[0] = jnp.sum(jnp.where(eye, db_col, 0.0), axis=0, keepdims=True)

    collects = c == 0
    in_own = jnp.logical_and(collects, own)

    def db_copy(m):
        return remote(db_send.at[0], db_recv.at[k], s_db.at[m], r_db.at[k], (m * H + head, 0))

    def db_each(action):
        for m in range(U // H):

            @pl.when(jnp.logical_not(jnp.logical_and(m * H + head == k, collects)))
            def _(m=m):
                action(db_copy(m))

    db_each(lambda copy: copy.start())

    @pl.when(in_own)
    def _():
        db_recv[k] = db_send[0]

    for jb in range(nt):
        acc = jnp.zeros((TB, W), jnp.float32)
        for ib in range(jb, nt):
            acc = acc + mm(wts[tile_at(ib, jb)], dat[:, ib * TB : (ib + 1) * TB], NT)
        g_send[1, jb * TB : (jb + 1) * TB] = acc.astype(jnp.bfloat16)
    for ib in range(nt):
        for p in range(per):
            r = ib * per + p
            g_send[2, r * W : (r + 1) * W] = (
                q_acc[ib][:, p * W : (p + 1) * W].T.astype(jnp.bfloat16)
            )
    half, most = H // 2, H - max(1, H // 4)
    for o in range(half):
        g_start(o)
    for o in range(half // 2):
        g_left(o)

    def dbs_copy(j):
        p = comp * H + j
        return remote(db_sum.at[0], db_mine.at[0], s_dbs.at[j], r_dbs, (p, ctx_of(e, p, H)))

    @pl.when(collects)
    def _():
        def db_wait(o):
            p = lax.rem(k + o, U)

            @pl.when(jnp.logical_not(jnp.logical_and(o == 0, in_own)))
            def _():
                arrived(db_recv.at[p], s_db.at[0], r_db.at[p])

        loop(0, U, db_wait)
        db_sum[0] = jnp.sum(db_recv[...], axis=0)
        for j in range(H):

            @pl.when(jnp.logical_not(jnp.logical_and(in_own, comp * H + j == k)))
            def _(j=j):
                dbs_copy(j).start()

    for o in range(half, most):
        g_start(o)
    for o in range(half // 2, half):
        g_left(o)

    @pl.when(in_own)
    def _():
        db_mine[0] = db_sum[0]

    @pl.when(jnp.logical_not(in_own))
    def _():
        arrived(db_mine.at[0], s_dbs.at[0], r_dbs)

    def dba_copy(o):
        cc = lax.rem(c + o, H)
        return remote(db_mine.at[0], db_all.at[c], s_dba.at[o], r_dba.at[c], (k, cc))

    loop(1, H, lambda o: dba_copy(o).start())
    db_all[c] = db_mine[0]

    for o in range(most, H):
        g_start(o)

    def dba_wait(o):
        cc = lax.rem(c + o, H)
        arrived(db_all.at[cc], s_dba.at[0], r_dba.at[cc])

    loop(1, H, dba_wait)

    def dba_put(cc):
        dbias[pl.ds(head_of(cc, k, H), 1), :] = db_all[cc]

    loop(0, H, dba_put)

    keep.wait()

    loop(0, U, lambda d: arrived(grads.at[d], s_g.at[0], r_g.at[d]))

    def ctx_end(o):
        cc = lax.rem(c + o, H)
        ref = out.at[:, rows(head_of(cc, k, H))]
        arrived(ref, s_out.at[0], r_out.at[cc])
        st_copy(o).wait_send()
        dba_copy(o).wait_send()
        cot_copy(o).wait_send()
        out_copy(o).wait_send()

    loop(1, H, ctx_end)

    @pl.when(jnp.logical_not(own))
    def _():
        in_copy(0).wait_send()

    loop(1, U, lambda o: in_copy(o).wait_send())
    for o in range(half, H):
        g_left(o)
    db_each(lambda copy: copy.wait_send())

    @pl.when(collects)
    def _():
        for j in range(H):

            @pl.when(jnp.logical_not(jnp.logical_and(in_own, comp * H + j == k)))
            def _(j=j):
                dbs_copy(j).wait_send()


def place(U, assign, out, grads, dbias, to_out, to_grads, to_bias, rows, blocks, bias, s_in, s_out):
    moves = [(out, rows, to_out), (dbias, bias, to_bias)]
    for d in range(U):
        moves.append((grads.at[d], blocks.at[d], to_grads.at[assign[d]]))
    loads = [
        pltpu.make_async_copy(src, via, s_in.at[n]) for n, (src, via, _) in enumerate(moves)
    ]
    stores = [
        pltpu.make_async_copy(via, dst, s_out.at[n]) for n, (_, via, dst) in enumerate(moves)
    ]
    for load in loads:
        load.start()
    for load, store in zip(loads, stores):
        load.wait()
        store.start()
    for store in stores:
        store.wait()


def on_device(uvqk, lengths, assignment, buckets, rel_bias, cotangent):
    U = assignment.shape[0]
    H = rel_bias.shape[0]
    LEN = buckets.shape[0]
    D = H * W
    nt = LEN // TB
    tiles = nt * (nt + 1) // 2
    vm = pl.BlockSpec(memory_space=pltpu.VMEM)
    hbm = pl.BlockSpec(memory_space=pltpu.HBM)
    bf, f32 = jnp.bfloat16, jnp.float32
    dma = pltpu.SemaphoreType.DMA
    shapes = [
        jax.ShapeDtypeStruct((W, D), bf),
        jax.ShapeDtypeStruct((U, W, W), bf),
        jax.ShapeDtypeStruct((H, W), f32),
    ]

    out, grads, dbias = pl.pallas_call(
        functools.partial(kernel, H, U),
        out_shape=shapes,
        in_specs=[hbm] * 6,
        out_specs=[hbm, hbm, vm],
        scratch_shapes=[
            pltpu.SMEM((U,), jnp.int32),
            pltpu.SMEM((U,), jnp.int32),
            pltpu.VMEM((U, W, W), bf),
            pltpu.VMEM((W, D), bf),
            pltpu.VMEM((1, LEN), jnp.int32),
            pltpu.VMEM((H, W), f32),
            pltpu.VMEM((U, W, W), bf),
            pltpu.VMEM((4, LEN, W), bf),
            pltpu.VMEM((LEN, W), bf),
            pltpu.VMEM((LEN, W), bf),
            pltpu.VMEM((4, LEN, W), bf),
            pltpu.VMEM((nt, TB, TB), f32),
            pltpu.VMEM((tiles, TB, TB), bf),
            pltpu.VMEM((tiles, TB, TB), f32),
            pltpu.VMEM((nt, TB, TB), f32),
            pltpu.VMEM((W, LEN), bf),
            pltpu.VMEM((W, LEN), bf),
            pltpu.VMEM((W, LEN), f32),
            pltpu.VMEM((W, LEN), f32),
            pltpu.VMEM((W, LEN), bf),
            pltpu.VMEM((H, 4, H, W), f32),
            pltpu.VMEM((4, H, W), f32),
            pltpu.VMEM((1, 1, W), f32),
            pltpu.VMEM((U, 1, W), f32),
            pltpu.VMEM((1, 1, W), f32),
            pltpu.VMEM((1, 1, W), f32),
            pltpu.VMEM((H, 1, W), f32),
            dma((6,)),
            dma((U,)),
            dma((4 * H,)),
            dma((H,)),
            dma((H,)),
            dma((H,)),
            dma((H,)),
            dma((H,)),
            dma((H,)),
            dma((4 * H,)),
            dma((U,)),
            dma((U // H,)),
            dma((U,)),
            dma((H,)),
            dma,
            dma((H,)),
            dma((H,)),
        ],
        compiler_params=pltpu.CompilerParams(
            collective_id=0, has_side_effects=True, vmem_limit_bytes=60 * 1024 * 1024
        ),
        name="layer",
    )(
        assignment,
        lengths,
        uvqk,
        cotangent.reshape(W, D),
        buckets.reshape(1, LEN),
        rel_bias,
    )
    out, grads, dbias = pl.pallas_call(
        functools.partial(place, U),
        out_shape=shapes,
        in_specs=[pl.BlockSpec(memory_space=pltpu.SMEM), hbm, hbm, hbm],
        out_specs=[hbm, hbm, hbm],
        scratch_shapes=[
            pltpu.VMEM((W, D), bf),
            pltpu.VMEM((U, W, W), bf),
            pltpu.VMEM((H, W), f32),
            dma((U + 2,)),
            dma((U + 2,)),
        ],
        compiler_params=pltpu.CompilerParams(vmem_limit_bytes=60 * 1024 * 1024),
        name="place",
    )(assignment, out, grads, dbias)
    return out.reshape(1, W, D), grads, dbias


def solution(mesh):
    in_specs = (P(None, "ctx", "dp"), P(), P(), P(), P(), P("dp", "ctx", None))
    out_specs = (P("dp", "ctx", None), P(None, "ctx", "dp"), P())
    return jax.shard_map(
        on_device, mesh=mesh, in_specs=in_specs, out_specs=out_specs, check_vma=False
    )
```

```python
import functools

import jax
import jax.numpy as jnp
from jax import lax
from jax.experimental import pallas as pl
from jax.experimental.pallas import tpu as pltpu
from jax.sharding import PartitionSpec as P

MESH = pl.DeviceIdType.MESH
Y = 4
TB = 256
W = 128
NN = (((1,), (0,)), ((), ()))
NT = (((1,), (1,)), ((), ()))


def mm(a, b, dims):
    return lax.dot_general(a, b, dims, preferred_element_type=jnp.float32)


def tile_at(ib, jb):
    return ib * (ib + 1) // 2 + jb


def ctx_of(h, p, H):
    if H != 8:
        return h
    y, b = lax.rem(h, 4), lax.div(h, 4)
    return lax.rem(y + 2 * b + lax.rem(p, 4), 4) * 2 + b


def head_of(c, p, H):
    if H != 8:
        return c
    x, b = lax.div(c, 2), lax.rem(c, 2)
    return b * 4 + lax.rem(x + 8 - 2 * b - lax.rem(p, 4), 4)


def kernel(
    H,
    U,
    assign_hbm,
    lengths_hbm,
    uvqk_hbm,
    cot_hbm,
    buckets_hbm,
    rel_hbm,
    out,
    grads,
    dbias,
    assign,
    lengths,
    uvqk,
    cot,
    buckets,
    rel,
    in_send,
    in_recv,
    cot_recv,
    out_send,
    g_send,
    toep,
    wts,
    dsl,
    diag,
    vt,
    kt,
    gt,
    at,
    dat,
    st_recv,
    st_send,
    db_send,
    db_recv,
    db_sum,
    db_mine,
    db_all,
    s_load,
    s_in,
    r_in,
    s_cot,
    r_cot,
    s_st,
    r_st,
    s_out,
    r_out,
    s_g,
    r_g,
    s_db,
    r_db,
    s_dbs,
    r_dbs,
    s_dba,
    r_dba,
):
    k = lax.axis_index("dp")
    c = lax.axis_index("ctx")
    e = lax.rem(k, H)
    comp = lax.div(k, H)
    head = head_of(c, k, H)
    own = e == head
    LEN = H * W
    nt = LEN // TB
    per = TB // W

    def rows(cc):
        if isinstance(cc, int):
            return pl.ds(cc * W, W)
        return pl.ds(pl.multiple_of(cc * W, W), W)

    def remote(src, dst, ss, rs, dev):
        return pltpu.make_async_remote_copy(
            src_ref=src, dst_ref=dst, send_sem=ss, recv_sem=rs, device_id=dev, device_id_type=MESH
        )

    def arrived(ref, ss, rs):
        remote(ref, ref, ss, rs, (k, c)).wait_recv()

    def loop(lo, hi, body):
        def step(i, _):
            body(i)
            return 0

        lax.fori_loop(lo, hi, step, 0)

    loads = [
        pltpu.make_async_copy(src, dst, s_load.at[n])
        for n, (src, dst) in enumerate(
            (
                (assign_hbm, assign),
                (uvqk_hbm, uvqk),
                (cot_hbm, cot),
                (lengths_hbm, lengths),
                (buckets_hbm, buckets),
                (rel_hbm, rel),
            )
        )
    ]
    for load in loads:
        load.start()
    barrier = pltpu.get_barrier_semaphore()

    for o in range(4 * H):
        far = (2, 3, 1, 0)[o // H]
        kk, cc = lax.rem(comp + far, 4) * H + head, lax.rem(c + o, H)
        if o % H or far:
            pl.semaphore_signal(barrier, inc=1, device_id=(kk, cc), device_id_type=MESH)
            continue

        @pl.when(kk != k)
        def _(kk=kk, cc=cc):
            pl.semaphore_signal(barrier, inc=1, device_id=(kk, cc), device_id_type=MESH)

    for o in range(1, H):
        pl.semaphore_signal(
            barrier, inc=1, device_id=(k, lax.rem(c + o, H)), device_id_type=MESH
        )

    for load in loads:
        load.wait()

    def arrange(p):
        in_send[p] = uvqk[assign[p]]

    loop(0, U, arrange)
    pl.semaphore_wait(barrier, U + H - 1 - own.astype(jnp.int32))

    z, y = lax.div(k, Y), lax.rem(k, Y)
    Z = U // Y

    def in_copy(o):
        dz, dy = (o // Y, o % Y) if isinstance(o, int) else (lax.div(o, Y), lax.rem(o, Y))
        p = lax.rem(z + dz, Z) * Y + lax.rem(y + dy, Y)
        return remote(
            in_send.at[p],
            in_recv.at[comp, rows(c)],
            s_in.at[o],
            r_in.at[comp * H + c],
            (p, ctx_of(e, p, H)),
        )

    @pl.when(jnp.logical_not(own))
    def _():
        in_copy(0).start()

    @pl.when(own)
    def _():
        pltpu.make_async_copy(
            in_send.at[k], in_recv.at[comp, rows(c)], r_in.at[comp * H + c]
        ).start()

    def cot_copy(o):
        cc = lax.rem(c + o, H)
        return remote(
            cot.at[:, rows(head_of(cc, k, H))],
            cot_recv.at[rows(c)],
            s_cot.at[o],
            r_cot.at[c],
            (k, cc),
        )

    ways = sorted(range(Z), key=lambda dz: dz)
    turn = [dz * Y + dy for dz in ways for dy in range(Y)]
    for n, o in enumerate(turn):
        if o > 0:
            in_copy(o).start()
        if n % Y == 1 and 0 < n // Y + 1 < H:
            cot_copy(n // Y + 1).start()
    for o in range(len(ways) + 1, H):
        cot_copy(o).start()
    cot_recv[rows(c), :] = cot[:, rows(head)]

    eye = lax.broadcasted_iota(jnp.int32, (W, W), 0) == lax.broadcasted_iota(
        jnp.int32, (W, W), 1
    )
    onehot = lax.broadcasted_iota(jnp.int32, (W, LEN), 0) == buckets[...]
    rel_col = jnp.sum(jnp.where(eye, rel[pl.ds(head, 1), :], 0.0), axis=1, keepdims=True)
    relative = jnp.sum(jnp.where(onehot, rel_col, 0.0), axis=0, keepdims=True)
    row8 = lax.broadcasted_iota(jnp.int32, (8, 2 * TB), 0)
    for m in range(nt):
        low = relative[:, m * TB : (m + 1) * TB]
        before = relative[:, (m - 1) * TB : m * TB] if m else low
        x = jnp.broadcast_to(jnp.concatenate([low, before], 1), (8, 2 * TB))
        for bit in (1, 2, 4):
            x = jnp.where((row8 & bit) != 0, pltpu.roll(x, bit, 1), x)
        size = 8
        while size < TB:
            x = jnp.concatenate([x, pltpu.roll(x, size, 1)], 0)
            size *= 2
        toep[m] = x[:, :TB]

    def come(which, cc):
        arrived(in_recv.at[which, rows(cc)], s_in.at[0], r_in.at[which * H + cc])

    def turned(which, cc):
        block = in_recv[which, cc * W : (cc + 1) * W].astype(jnp.float32)
        return block.T.astype(jnp.bfloat16)

    user_len = lengths[assign[k]]
    for which in (1, 2, 3):
        for cc in range(H):
            come(which, cc)
    for cc in range(H):
        vt[:, cc * W : (cc + 1) * W] = turned(1, cc)
    key_at = lax.broadcasted_iota(jnp.int32, (TB, TB), 0)
    for ib in range(nt):
        query_at = lax.broadcasted_iota(jnp.int32, (1, TB), 1) + ib * TB
        limit = jnp.where(query_at < user_len, query_at, -1)
        q = in_recv[2, ib * TB : (ib + 1) * TB]
        acc = jnp.zeros((W, TB), jnp.float32)
        for jb in range(ib + 1):
            t = tile_at(ib, jb)
            score = mm(in_recv[3, jb * TB : (jb + 1) * TB], q, NT) + toep[ib - jb]
            live = key_at <= limit - jb * TB
            sig = 0.5 + 0.5 * jnp.tanh(0.5 * score)
            weight = score * sig
            slope = sig + weight * (1.0 - sig)
            wb = jnp.where(live, weight, 0.0).astype(jnp.bfloat16)
            wts[t] = wb
            dsl[t] = jnp.where(live, slope, 0.0)
            acc = acc + mm(vt[:, jb * TB : (jb + 1) * TB], wb, NN)
        at[:, ib * TB : (ib + 1) * TB] = acc

    gsums = []
    for cc in range(H):
        blk = slice(cc * W, (cc + 1) * W)
        come(0, cc)

        @pl.when(c != cc)
        def _(cc=cc):
            arrived(cot_recv.at[rows(cc)], s_cot.at[0], r_cot.at[cc])

        grad = (cot_recv[blk].astype(jnp.float32) * in_recv[0, blk].astype(jnp.float32)).T
        gt[:, blk] = grad
        gsums.append(jnp.sum(grad, axis=0, keepdims=True))

    means, spreads, gdots = [], [], []
    for r in range(H):
        blk = slice(r * W, (r + 1) * W)
        a = at[:, blk]
        mean = jnp.sum(a, axis=0, keepdims=True) * (1.0 / W)
        centered = a - mean
        means.append(mean)
        spreads.append(jnp.sum(centered * centered, axis=0, keepdims=True))
        gdots.append(jnp.sum(gt[:, blk] * centered, axis=0, keepdims=True))
    for n, rows_of in enumerate((means, spreads, gsums, gdots)):
        st_send[n] = jnp.concatenate(rows_of, 0)

    def st_copy(o):
        cc = lax.rem(c + o, H)
        return remote(st_send, st_recv.at[c], s_st.at[o], r_st.at[c], (k, cc))

    loop(1, H, lambda o: st_copy(o).start())
    st_recv[c] = st_send[...]

    for cc in range(H):
        kt[:, cc * W : (cc + 1) * W] = turned(3, cc)

    def st_wait(o):
        cc = lax.rem(c + o, H)
        arrived(st_recv.at[cc], s_st.at[0], r_st.at[cc])

    loop(1, H, st_wait)

    D = H * W
    mean = st_recv[0, 0]
    for h in range(1, H):
        mean = mean + st_recv[h, 0]
    mean = mean * (1.0 / H)
    square = jnp.zeros_like(mean)
    g_total = jnp.zeros_like(mean)
    gn_total = jnp.zeros_like(mean)
    for h in range(H):
        off = st_recv[h, 0] - mean
        square = square + (st_recv[h, 1] + W * (off * off))
        g_total = g_total + st_recv[h, 2]
        gn_total = gn_total + (st_recv[h, 3] + off * st_recv[h, 2])
    inv = lax.rsqrt(square * (1.0 / D) + 1e-05)
    g_mean = g_total * (1.0 / D)
    gn_mean = gn_total * inv * (1.0 / D)
    for r in range(H):
        blk = slice(r * W, (r + 1) * W)
        row = slice(r, r + 1)
        normed = (at[:, blk] - mean[row]) * inv[row]
        dat[:, blk] = (
            (gt[:, blk] - g_mean[row] - normed * gn_mean[row]) * inv[row]
        ).astype(jnp.bfloat16)
        natural = normed.T
        out_send[blk] = (natural * in_recv[0, blk].astype(jnp.float32)).astype(jnp.bfloat16)
        g_send[0, blk] = (natural * cot_recv[blk].astype(jnp.float32)).astype(jnp.bfloat16)

    def g_copy(which, o):
        cc = lax.rem(c + o, H)
        return remote(
            g_send.at[which, rows(cc)],
            grads.at[k],
            s_g.at[which * H + o],
            r_g.at[k],
            (which * H + head, cc),
        )

    early = range(1, H // 2 + 1)

    def g_start(o):
        for n in range(4):
            which = lax.rem(comp + n, 4)
            copy = g_copy(which, o)
            if o in early:

                @pl.when(which != 0)
                def _(copy=copy):
                    copy.start()

                continue
            if o > 0:
                copy.start()
                continue
            mine = which * H + head == k

            @pl.when(jnp.logical_not(mine))
            def _(copy=copy):
                copy.start()

            @pl.when(mine)
            def _(which=which):
                pltpu.make_async_copy(g_send.at[which, rows(c)], grads.at[k], r_g.at[k]).start()

    def g_left(o):
        for which in range(4):
            if o > 0:
                g_copy(which, o).wait_send()
                continue

            @pl.when(which * H + head != k)
            def _(which=which):
                g_copy(which, 0).wait_send()

    def out_copy(o):
        cc = lax.rem(c + o, H)
        return remote(
            out_send.at[rows(cc)], out.at[:, rows(head)], s_out.at[o], r_out.at[c], (k, cc)
        )

    for o in early:
        g_copy(0, o).start()
        out_copy(o).start()
    keep = pltpu.make_async_copy(out_send.at[rows(c)], out.at[:, rows(head)], s_out.at[0])
    keep.start()

    q_acc = [jnp.zeros((W, TB), jnp.float32) for _ in range(nt)]
    for jb in range(nt):
        value = in_recv[1, jb * TB : (jb + 1) * TB]
        acc = jnp.zeros((TB, W), jnp.float32)
        for ib in range(jb, nt):
            t = tile_at(ib, jb)
            ds = mm(value, dat[:, ib * TB : (ib + 1) * TB], NN) * dsl[t]
            if jb == 0:
                diag[ib - jb] = ds
            else:
                diag[ib - jb] += ds
            dsb = ds.astype(jnp.bfloat16)
            acc = acc + mm(dsb, in_recv[2, ib * TB : (ib + 1) * TB], NN)
            q_acc[ib] = q_acc[ib] + mm(kt[:, jb * TB : (jb + 1) * TB], dsb, NN)
        g_send[3, jb * TB : (jb + 1) * TB] = acc.astype(jnp.bfloat16)
    sheared = []
    for m in range(nt):
        x = jnp.concatenate([diag[m], jnp.zeros((TB, TB), jnp.float32)], 1)
        size = TB
        while size > 8:
            size //= 2
            x = x[:size] + pltpu.roll(x[size:], 2 * TB - size, 1)
        for bit in (1, 2, 4):
            x = jnp.where((row8 & bit) != 0, pltpu.roll(x, 2 * TB - bit, 1), x)
        sheared.append(jnp.sum(x, axis=0, keepdims=True))
    by_distance = []
    for m in range(nt):
        part = sheared[m][:, :TB]
        if m + 1 < nt:
            part = part + sheared[m + 1][:, TB:]
        by_distance.append(part)
    by_distance = jnp.concatenate(by_distance, 1)
    db_col = jnp.sum(jnp.where(onehot, by_distance, 0.0), axis=1, keepdims=True)
    db_send[0] = jnp.sum(jnp.where(eye, db_col, 0.0), axis=0, keepdims=True)

    collects = c == 0
    in_own = jnp.logical_and(collects, own)

    def db_copy(m):
        return remote(db_send.at[0], db_recv.at[k], s_db.at[m], r_db.at[k], (m * H + head, 0))

    def db_each(action):
        for m in range(U // H):

            @pl.when(jnp.logical_not(jnp.logical_and(m * H + head == k, collects)))
            def _(m=m):
                action(db_copy(m))

    db_each(lambda copy: copy.start())

    @pl.when(in_own)
    def _():
        db_recv[k] = db_send[0]

    for jb in range(nt):
        acc = jnp.zeros((TB, W), jnp.float32)
        for ib in range(jb, nt):
            acc = acc + mm(wts[tile_at(ib, jb)], dat[:, ib * TB : (ib + 1) * TB], NT)
        g_send[1, jb * TB : (jb + 1) * TB] = acc.astype(jnp.bfloat16)
    for ib in range(nt):
        for p in range(per):
            r = ib * per + p
            g_send[2, r * W : (r + 1) * W] = (
                q_acc[ib][:, p * W : (p + 1) * W].T.astype(jnp.bfloat16)
            )
    for o in range(len(early) + 1, H):
        out_copy(o).start()

    half, most = H // 2, H - max(1, H // 4)
    for o in range(half):
        g_start(o)
    for o in range(half // 2):
        g_left(o)

    def dbs_copy(j):
        p = comp * H + j
        return remote(db_sum.at[0], db_mine.at[0], s_dbs.at[j], r_dbs, (p, ctx_of(e, p, H)))

    @pl.when(collects)
    def _():
        def db_wait(o):
            p = lax.rem(k + o, U)

            @pl.when(jnp.logical_not(jnp.logical_and(o == 0, in_own)))
            def _():
                arrived(db_recv.at[p], s_db.at[0], r_db.at[p])

        loop(0, U, db_wait)
        db_sum[0] = jnp.sum(db_recv[...], axis=0)
        for j in range(H):

            @pl.when(jnp.logical_not(jnp.logical_and(in_own, comp * H + j == k)))
            def _(j=j):
                dbs_copy(j).start()

    for o in range(half, most):
        g_start(o)
    for o in range(half // 2, half):
        g_left(o)

    @pl.when(in_own)
    def _():
        db_mine[0] = db_sum[0]

    @pl.when(jnp.logical_not(in_own))
    def _():
        arrived(db_mine.at[0], s_dbs.at[0], r_dbs)

    def dba_copy(o):
        cc = lax.rem(c + o, H)
        return remote(db_mine.at[0], db_all.at[c], s_dba.at[o], r_dba.at[c], (k, cc))

    loop(1, H, lambda o: dba_copy(o).start())
    db_all[c] = db_mine[0]

    for o in range(most, H):
        g_start(o)

    def dba_wait(o):
        cc = lax.rem(c + o, H)
        arrived(db_all.at[cc], s_dba.at[0], r_dba.at[cc])

    loop(1, H, dba_wait)

    def dba_put(cc):
        dbias[pl.ds(head_of(cc, k, H), 1), :] = db_all[cc]

    loop(0, H, dba_put)

    keep.wait()

    loop(0, U, lambda d: arrived(grads.at[d], s_g.at[0], r_g.at[d]))

    def ctx_end(o):
        cc = lax.rem(c + o, H)
        ref = out.at[:, rows(head_of(cc, k, H))]
        arrived(ref, s_out.at[0], r_out.at[cc])
        st_copy(o).wait_send()
        dba_copy(o).wait_send()
        cot_copy(o).wait_send()
        out_copy(o).wait_send()

    loop(1, H, ctx_end)

    @pl.when(jnp.logical_not(own))
    def _():
        in_copy(0).wait_send()

    loop(1, U, lambda o: in_copy(o).wait_send())
    for o in range(half, H):
        g_left(o)
    db_each(lambda copy: copy.wait_send())

    @pl.when(collects)
    def _():
        for j in range(H):

            @pl.when(jnp.logical_not(jnp.logical_and(in_own, comp * H + j == k)))
            def _(j=j):
                dbs_copy(j).wait_send()


def place(U, assign, out, grads, dbias, to_out, to_grads, to_bias, rows, blocks, bias, s_in, s_out):
    parts = 4
    some = U // parts

    def load(n):
        part = pl.ds(n * some, some)
        return pltpu.make_async_copy(grads.at[part], blocks.at[part], s_in.at[n])

    def store(d):
        return pltpu.make_async_copy(blocks.at[d], to_grads.at[assign[d]], s_out.at[d])

    ends = [(out, rows, to_out), (dbias, bias, to_bias)]
    first = [pltpu.make_async_copy(a, b, s_in.at[parts + n]) for n, (a, b, _) in enumerate(ends)]
    last = [pltpu.make_async_copy(b, c, s_out.at[U + n]) for n, (_, b, c) in enumerate(ends)]
    for n in range(parts):
        load(n).start()
    for copy in first:
        copy.start()
    for n in range(parts):
        load(n).wait()
        for d in range(n * some, (n + 1) * some):
            store(d).start()
    for a, b in zip(first, last):
        a.wait()
        b.start()
    for d in range(U):
        store(d).wait()
    for copy in last:
        copy.wait()


def on_device(uvqk, lengths, assignment, buckets, rel_bias, cotangent):
    U = assignment.shape[0]
    H = rel_bias.shape[0]
    LEN = buckets.shape[0]
    D = H * W
    nt = LEN // TB
    tiles = nt * (nt + 1) // 2
    vm = pl.BlockSpec(memory_space=pltpu.VMEM)
    hbm = pl.BlockSpec(memory_space=pltpu.HBM)
    bf, f32 = jnp.bfloat16, jnp.float32
    dma = pltpu.SemaphoreType.DMA
    shapes = [
        jax.ShapeDtypeStruct((W, D), bf),
        jax.ShapeDtypeStruct((U, W, W), bf),
        jax.ShapeDtypeStruct((H, W), f32),
    ]

    out, grads, dbias = pl.pallas_call(
        functools.partial(kernel, H, U),
        out_shape=shapes,
        in_specs=[hbm] * 6,
        out_specs=[hbm, hbm, vm],
        scratch_shapes=[
            pltpu.SMEM((U,), jnp.int32),
            pltpu.SMEM((U,), jnp.int32),
            pltpu.VMEM((U, W, W), bf),
            pltpu.VMEM((W, D), bf),
            pltpu.VMEM((1, LEN), jnp.int32),
            pltpu.VMEM((H, W), f32),
            pltpu.VMEM((U, W, W), bf),
            pltpu.VMEM((4, LEN, W), bf),
            pltpu.VMEM((LEN, W), bf),
            pltpu.VMEM((LEN, W), bf),
            pltpu.VMEM((4, LEN, W), bf),
            pltpu.VMEM((nt, TB, TB), f32),
            pltpu.VMEM((tiles, TB, TB), bf),
            pltpu.VMEM((tiles, TB, TB), f32),
            pltpu.VMEM((nt, TB, TB), f32),
            pltpu.VMEM((W, LEN), bf),
            pltpu.VMEM((W, LEN), bf),
            pltpu.VMEM((W, LEN), f32),
            pltpu.VMEM((W, LEN), f32),
            pltpu.VMEM((W, LEN), bf),
            pltpu.VMEM((H, 4, H, W), f32),
            pltpu.VMEM((4, H, W), f32),
            pltpu.VMEM((1, 1, W), f32),
            pltpu.VMEM((U, 1, W), f32),
            pltpu.VMEM((1, 1, W), f32),
            pltpu.VMEM((1, 1, W), f32),
            pltpu.VMEM((H, 1, W), f32),
            dma((6,)),
            dma((U,)),
            dma((4 * H,)),
            dma((H,)),
            dma((H,)),
            dma((H,)),
            dma((H,)),
            dma((H,)),
            dma((H,)),
            dma((4 * H,)),
            dma((U,)),
            dma((U // H,)),
            dma((U,)),
            dma((H,)),
            dma,
            dma((H,)),
            dma((H,)),
        ],
        compiler_params=pltpu.CompilerParams(
            collective_id=0, has_side_effects=True, vmem_limit_bytes=60 * 1024 * 1024
        ),
        name="layer",
    )(
        assignment,
        lengths,
        uvqk,
        cotangent.reshape(W, D),
        buckets.reshape(1, LEN),
        rel_bias,
    )
    out, grads, dbias = pl.pallas_call(
        functools.partial(place, U),
        out_shape=shapes,
        in_specs=[pl.BlockSpec(memory_space=pltpu.SMEM), hbm, hbm, hbm],
        out_specs=[hbm, hbm, hbm],
        scratch_shapes=[
            pltpu.VMEM((W, D), bf),
            pltpu.VMEM((U, W, W), bf),
            pltpu.VMEM((H, W), f32),
            dma((U + 2,)),
            dma((U + 2,)),
        ],
        compiler_params=pltpu.CompilerParams(vmem_limit_bytes=60 * 1024 * 1024),
        name="place",
    )(assignment, out, grads, dbias)
    return out.reshape(1, W, D), grads, dbias


def solution(mesh):
    in_specs = (P(None, "ctx", "dp"), P(), P(), P(), P(), P("dp", "ctx", None))
    out_specs = (P("dp", "ctx", None), P(None, "ctx", "dp"), P())
    return jax.shard_map(
        on_device, mesh=mesh, in_specs=in_specs, out_specs=out_specs, check_vma=False
    )
```

```python
import functools

import jax
import jax.numpy as jnp
from jax import lax
from jax.experimental import pallas as pl
from jax.experimental.pallas import tpu as pltpu
from jax.sharding import PartitionSpec as P

MESH = pl.DeviceIdType.MESH
Y = 4
TB = 256
W = 128
NN = (((1,), (0,)), ((), ()))
NT = (((1,), (1,)), ((), ()))


def mm(a, b, dims):
    return lax.dot_general(a, b, dims, preferred_element_type=jnp.float32)


def tile_at(ib, jb):
    return ib * (ib + 1) // 2 + jb


def ctx_of(h, p, H):
    if H != 8:
        return h
    y, b = lax.rem(h, 4), lax.div(h, 4)
    return lax.rem(y + 2 * b + lax.rem(p, 4), 4) * 2 + b


def head_of(c, p, H):
    if H != 8:
        return c
    x, b = lax.div(c, 2), lax.rem(c, 2)
    return b * 4 + lax.rem(x + 8 - 2 * b - lax.rem(p, 4), 4)


def kernel(
    H,
    U,
    assign_hbm,
    lengths_hbm,
    uvqk_hbm,
    cot_hbm,
    buckets_hbm,
    rel_hbm,
    out,
    grads,
    dbias_hbm,
    assign,
    lengths,
    uvqk,
    cot,
    buckets,
    rel,
    dbias,
    in_send,
    in_recv,
    cot_recv,
    out_send,
    g_send,
    toep,
    wts,
    dsl,
    diag,
    vt,
    kt,
    gt,
    at,
    dat,
    st_recv,
    st_send,
    db_send,
    db_recv,
    db_sum,
    db_mine,
    db_all,
    s_load,
    s_in,
    r_in,
    s_cot,
    r_cot,
    s_st,
    r_st,
    s_out,
    r_out,
    s_g,
    r_g,
    s_db,
    r_db,
    s_dbs,
    r_dbs,
    s_dba,
    r_dba,
):
    k = lax.axis_index("dp")
    c = lax.axis_index("ctx")
    e = lax.rem(k, H)
    comp = lax.div(k, H)
    head = head_of(c, k, H)
    own = e == head
    LEN = H * W
    nt = LEN // TB
    per = TB // W

    def rows(cc):
        if isinstance(cc, int):
            return pl.ds(cc * W, W)
        return pl.ds(pl.multiple_of(cc * W, W), W)

    def remote(src, dst, ss, rs, dev):
        return pltpu.make_async_remote_copy(
            src_ref=src, dst_ref=dst, send_sem=ss, recv_sem=rs, device_id=dev, device_id_type=MESH
        )

    def arrived(ref, ss, rs):
        remote(ref, ref, ss, rs, (k, c)).wait_recv()

    def loop(lo, hi, body):
        def step(i, _):
            body(i)
            return 0

        lax.fori_loop(lo, hi, step, 0)

    loads = [
        pltpu.make_async_copy(src, dst, s_load.at[n])
        for n, (src, dst) in enumerate(
            (
                (assign_hbm, assign),
                (uvqk_hbm, uvqk),
                (cot_hbm, cot),
                (lengths_hbm, lengths),
                (buckets_hbm, buckets),
                (rel_hbm, rel),
            )
        )
    ]
    for load in loads:
        load.start()
    barrier = pltpu.get_barrier_semaphore()

    for o in range(4 * H):
        far = (2, 3, 1, 0)[o // H]
        kk, cc = lax.rem(comp + far, 4) * H + head, lax.rem(c + o, H)
        if o % H or far:
            pl.semaphore_signal(barrier, inc=1, device_id=(kk, cc), device_id_type=MESH)
            continue

        @pl.when(kk != k)
        def _(kk=kk, cc=cc):
            pl.semaphore_signal(barrier, inc=1, device_id=(kk, cc), device_id_type=MESH)

    for o in range(1, H):
        pl.semaphore_signal(
            barrier, inc=1, device_id=(k, lax.rem(c + o, H)), device_id_type=MESH
        )

    for load in loads:
        load.wait()

    def arrange(p):
        in_send[p] = uvqk[assign[p]]

    loop(0, U, arrange)
    pl.semaphore_wait(barrier, U + H - 1 - own.astype(jnp.int32))

    z, y = lax.div(k, Y), lax.rem(k, Y)
    Z = U // Y

    def in_copy(o):
        dz, dy = (o // Y, o % Y) if isinstance(o, int) else (lax.div(o, Y), lax.rem(o, Y))
        p = lax.rem(z + dz, Z) * Y + lax.rem(y + dy, Y)
        return remote(
            in_send.at[p],
            in_recv.at[comp, rows(c)],
            s_in.at[o],
            r_in.at[comp * H + c],
            (p, ctx_of(e, p, H)),
        )

    @pl.when(jnp.logical_not(own))
    def _():
        in_copy(0).start()

    @pl.when(own)
    def _():
        pltpu.make_async_copy(
            in_send.at[k], in_recv.at[comp, rows(c)], r_in.at[comp * H + c]
        ).start()

    def cot_copy(o):
        cc = lax.rem(c + o, H)
        return remote(
            cot.at[:, rows(head_of(cc, k, H))],
            cot_recv.at[rows(c)],
            s_cot.at[o],
            r_cot.at[c],
            (k, cc),
        )

    ways = sorted(range(Z), key=lambda dz: dz)
    turn = [dz * Y + dy for dz in ways for dy in range(Y)]
    for n, o in enumerate(turn):
        if o > 0:
            in_copy(o).start()
        if n % Y == 1 and 0 < n // Y + 1 < H:
            cot_copy(n // Y + 1).start()
    for o in range(len(ways) + 1, H):
        cot_copy(o).start()
    cot_recv[rows(c), :] = cot[:, rows(head)]

    eye = lax.broadcasted_iota(jnp.int32, (W, W), 0) == lax.broadcasted_iota(
        jnp.int32, (W, W), 1
    )
    onehot = lax.broadcasted_iota(jnp.int32, (W, LEN), 0) == buckets[...]
    rel_col = jnp.sum(jnp.where(eye, rel[pl.ds(head, 1), :], 0.0), axis=1, keepdims=True)
    relative = jnp.sum(jnp.where(onehot, rel_col, 0.0), axis=0, keepdims=True)
    row8 = lax.broadcasted_iota(jnp.int32, (8, 2 * TB), 0)
    for m in range(nt):
        low = relative[:, m * TB : (m + 1) * TB]
        before = relative[:, (m - 1) * TB : m * TB] if m else low
        x = jnp.broadcast_to(jnp.concatenate([low, before], 1), (8, 2 * TB))
        for bit in (1, 2, 4):
            x = jnp.where((row8 & bit) != 0, pltpu.roll(x, bit, 1), x)
        size = 8
        while size < TB:
            x = jnp.concatenate([x, pltpu.roll(x, size, 1)], 0)
            size *= 2
        toep[m] = x[:, :TB]

    def come(which, cc):
        arrived(in_recv.at[which, rows(cc)], s_in.at[0], r_in.at[which * H + cc])

    def turned(which, cc):
        block = in_recv[which, cc * W : (cc + 1) * W].astype(jnp.float32)
        return block.T.astype(jnp.bfloat16)

    user_len = lengths[assign[k]]
    for which in (1, 2, 3):
        for cc in range(H):
            come(which, cc)
    for cc in range(H):
        vt[:, cc * W : (cc + 1) * W] = turned(1, cc)
    key_at = lax.broadcasted_iota(jnp.int32, (TB, TB), 0)
    for ib in range(nt):
        query_at = lax.broadcasted_iota(jnp.int32, (1, TB), 1) + ib * TB
        limit = jnp.where(query_at < user_len, query_at, -1)
        q = in_recv[2, ib * TB : (ib + 1) * TB]
        acc = jnp.zeros((W, TB), jnp.float32)
        for jb in range(ib + 1):
            t = tile_at(ib, jb)
            score = mm(in_recv[3, jb * TB : (jb + 1) * TB], q, NT) + toep[ib - jb]
            live = key_at <= limit - jb * TB
            sig = 0.5 + 0.5 * jnp.tanh(0.5 * score)
            weight = score * sig
            slope = sig + weight * (1.0 - sig)
            wb = jnp.where(live, weight, 0.0).astype(jnp.bfloat16)
            wts[t] = wb
            dsl[t] = jnp.where(live, slope, 0.0)
            acc = acc + mm(vt[:, jb * TB : (jb + 1) * TB], wb, NN)
        at[:, ib * TB : (ib + 1) * TB] = acc

    gsums = []
    for cc in range(H):
        blk = slice(cc * W, (cc + 1) * W)
        come(0, cc)

        @pl.when(c != cc)
        def _(cc=cc):
            arrived(cot_recv.at[rows(cc)], s_cot.at[0], r_cot.at[cc])

        grad = (cot_recv[blk].astype(jnp.float32) * in_recv[0, blk].astype(jnp.float32)).T
        gt[:, blk] = grad
        gsums.append(jnp.sum(grad, axis=0, keepdims=True))

    means, spreads, gdots = [], [], []
    for r in range(H):
        blk = slice(r * W, (r + 1) * W)
        a = at[:, blk]
        mean = jnp.sum(a, axis=0, keepdims=True) * (1.0 / W)
        centered = a - mean
        means.append(mean)
        spreads.append(jnp.sum(centered * centered, axis=0, keepdims=True))
        gdots.append(jnp.sum(gt[:, blk] * centered, axis=0, keepdims=True))
    for n, rows_of in enumerate((means, spreads, gsums, gdots)):
        st_send[n] = jnp.concatenate(rows_of, 0)

    def st_copy(o):
        cc = lax.rem(c + o, H)
        return remote(st_send, st_recv.at[c], s_st.at[o], r_st.at[c], (k, cc))

    loop(1, H, lambda o: st_copy(o).start())
    st_recv[c] = st_send[...]

    for cc in range(H):
        kt[:, cc * W : (cc + 1) * W] = turned(3, cc)

    def st_wait(o):
        cc = lax.rem(c + o, H)
        arrived(st_recv.at[cc], s_st.at[0], r_st.at[cc])

    loop(1, H, st_wait)

    D = H * W
    mean = st_recv[0, 0]
    for h in range(1, H):
        mean = mean + st_recv[h, 0]
    mean = mean * (1.0 / H)
    square = jnp.zeros_like(mean)
    g_total = jnp.zeros_like(mean)
    gn_total = jnp.zeros_like(mean)
    for h in range(H):
        off = st_recv[h, 0] - mean
        square = square + (st_recv[h, 1] + W * (off * off))
        g_total = g_total + st_recv[h, 2]
        gn_total = gn_total + (st_recv[h, 3] + off * st_recv[h, 2])
    inv = lax.rsqrt(square * (1.0 / D) + 1e-05)
    g_mean = g_total * (1.0 / D)
    gn_mean = gn_total * inv * (1.0 / D)
    for r in range(H):
        blk = slice(r * W, (r + 1) * W)
        row = slice(r, r + 1)
        normed = (at[:, blk] - mean[row]) * inv[row]
        dat[:, blk] = (
            (gt[:, blk] - g_mean[row] - normed * gn_mean[row]) * inv[row]
        ).astype(jnp.bfloat16)
        natural = normed.T
        out_send[blk] = (natural * in_recv[0, blk].astype(jnp.float32)).astype(jnp.bfloat16)
        g_send[0, blk] = (natural * cot_recv[blk].astype(jnp.float32)).astype(jnp.bfloat16)

    def g_copy(which, o):
        cc = lax.rem(c + o, H)
        return remote(
            g_send.at[which, rows(cc)],
            grads.at[k],
            s_g.at[which * H + o],
            r_g.at[k],
            (which * H + head, cc),
        )

    early = range(1, max(1, H // 4) + 1)

    def g_start(o):
        for n in range(4):
            which = lax.rem(comp + n, 4)
            copy = g_copy(which, o)
            if o in early:

                @pl.when(which != 0)
                def _(copy=copy):
                    copy.start()

                continue
            if o > 0:
                copy.start()
                continue
            mine = which * H + head == k

            @pl.when(jnp.logical_not(mine))
            def _(copy=copy):
                copy.start()

            @pl.when(mine)
            def _(which=which):
                pltpu.make_async_copy(g_send.at[which, rows(c)], grads.at[k], r_g.at[k]).start()

    def g_left(o):
        for which in range(4):
            if o > 0:
                g_copy(which, o).wait_send()
                continue

            @pl.when(which * H + head != k)
            def _(which=which):
                g_copy(which, 0).wait_send()

    def out_copy(o):
        cc = lax.rem(c + o, H)
        return remote(
            out_send.at[rows(cc)], out.at[:, rows(head)], s_out.at[o], r_out.at[c], (k, cc)
        )

    for o in early:
        g_copy(0, o).start()
        out_copy(o).start()
    keep = pltpu.make_async_copy(out_send.at[rows(c)], out.at[:, rows(head)], s_out.at[0])
    keep.start()

    q_acc = [jnp.zeros((W, TB), jnp.float32) for _ in range(nt)]
    for jb in range(nt):
        value = in_recv[1, jb * TB : (jb + 1) * TB]
        acc = jnp.zeros((TB, W), jnp.float32)
        for ib in range(jb, nt):
            t = tile_at(ib, jb)
            ds = mm(value, dat[:, ib * TB : (ib + 1) * TB], NN) * dsl[t]
            if jb == 0:
                diag[ib - jb] = ds
            else:
                diag[ib - jb] += ds
            dsb = ds.astype(jnp.bfloat16)
            acc = acc + mm(dsb, in_recv[2, ib * TB : (ib + 1) * TB], NN)
            q_acc[ib] = q_acc[ib] + mm(kt[:, jb * TB : (jb + 1) * TB], dsb, NN)
        g_send[3, jb * TB : (jb + 1) * TB] = acc.astype(jnp.bfloat16)
    sheared = []
    for m in range(nt):
        x = jnp.concatenate([diag[m], jnp.zeros((TB, TB), jnp.float32)], 1)
        size = TB
        while size > 8:
            size //= 2
            x = x[:size] + pltpu.roll(x[size:], 2 * TB - size, 1)
        for bit in (1, 2, 4):
            x = jnp.where((row8 & bit) != 0, pltpu.roll(x, 2 * TB - bit, 1), x)
        sheared.append(jnp.sum(x, axis=0, keepdims=True))
    by_distance = []
    for m in range(nt):
        part = sheared[m][:, :TB]
        if m + 1 < nt:
            part = part + sheared[m + 1][:, TB:]
        by_distance.append(part)
    by_distance = jnp.concatenate(by_distance, 1)
    db_col = jnp.sum(jnp.where(onehot, by_distance, 0.0), axis=1, keepdims=True)
    db_send[0] = jnp.sum(jnp.where(eye, db_col, 0.0), axis=0, keepdims=True)

    collects = c == 0
    in_own = jnp.logical_and(collects, own)

    def db_copy(m):
        return remote(db_send.at[0], db_recv.at[k], s_db.at[m], r_db.at[k], (m * H + head, 0))

    def db_each(action):
        for m in range(U // H):

            @pl.when(jnp.logical_not(jnp.logical_and(m * H + head == k, collects)))
            def _(m=m):
                action(db_copy(m))

    db_each(lambda copy: copy.start())

    @pl.when(in_own)
    def _():
        db_recv[k] = db_send[0]

    for jb in range(nt):
        acc = jnp.zeros((TB, W), jnp.float32)
        for ib in range(jb, nt):
            acc = acc + mm(wts[tile_at(ib, jb)], dat[:, ib * TB : (ib + 1) * TB], NT)
        g_send[1, jb * TB : (jb + 1) * TB] = acc.astype(jnp.bfloat16)
    for ib in range(nt):
        for p in range(per):
            r = ib * per + p
            g_send[2, r * W : (r + 1) * W] = (
                q_acc[ib][:, p * W : (p + 1) * W].T.astype(jnp.bfloat16)
            )
    for o in range(len(early) + 1, H):
        out_copy(o).start()

    half, most = H // 2, H - max(1, H // 4)
    for o in range(half):
        g_start(o)
    for o in range(half // 2):
        g_left(o)

    def dbs_copy(j):
        p = comp * H + j
        return remote(db_sum.at[0], db_mine.at[0], s_dbs.at[j], r_dbs, (p, ctx_of(e, p, H)))

    @pl.when(collects)
    def _():
        def db_wait(o):
            p = lax.rem(k + o, U)

            @pl.when(jnp.logical_not(jnp.logical_and(o == 0, in_own)))
            def _():
                arrived(db_recv.at[p], s_db.at[0], r_db.at[p])

        loop(0, U, db_wait)
        db_sum[0] = jnp.sum(db_recv[...], axis=0)
        for j in range(H):

            @pl.when(jnp.logical_not(jnp.logical_and(in_own, comp * H + j == k)))
            def _(j=j):
                dbs_copy(j).start()

    for o in range(half, most):
        g_start(o)
    for o in range(half // 2, half):
        g_left(o)

    @pl.when(in_own)
    def _():
        db_mine[0] = db_sum[0]

    @pl.when(jnp.logical_not(in_own))
    def _():
        arrived(db_mine.at[0], s_dbs.at[0], r_dbs)

    def dba_copy(o):
        cc = lax.rem(c + o, H)
        return remote(db_mine.at[0], db_all.at[c], s_dba.at[o], r_dba.at[c], (k, cc))

    loop(1, H, lambda o: dba_copy(o).start())
    db_all[c] = db_mine[0]

    for o in range(most, H):
        g_start(o)

    def dba_wait(o):
        cc = lax.rem(c + o, H)
        arrived(db_all.at[cc], s_dba.at[0], r_dba.at[cc])

    loop(1, H, dba_wait)

    def dba_put(cc):
        dbias[pl.ds(head_of(cc, k, H), 1), :] = db_all[cc]

    loop(0, H, dba_put)
    put = pltpu.make_async_copy(dbias, dbias_hbm, s_load.at[0])
    put.start()

    keep.wait()
    put.wait()

    loop(0, U, lambda d: arrived(grads.at[d], s_g.at[0], r_g.at[d]))

    def ctx_end(o):
        cc = lax.rem(c + o, H)
        ref = out.at[:, rows(head_of(cc, k, H))]
        arrived(ref, s_out.at[0], r_out.at[cc])
        st_copy(o).wait_send()
        dba_copy(o).wait_send()
        cot_copy(o).wait_send()
        out_copy(o).wait_send()

    loop(1, H, ctx_end)

    @pl.when(jnp.logical_not(own))
    def _():
        in_copy(0).wait_send()

    loop(1, U, lambda o: in_copy(o).wait_send())
    for o in range(half, H):
        g_left(o)
    db_each(lambda copy: copy.wait_send())

    @pl.when(collects)
    def _():
        for j in range(H):

            @pl.when(jnp.logical_not(jnp.logical_and(in_own, comp * H + j == k)))
            def _(j=j):
                dbs_copy(j).wait_send()


def place(
    U, users, out, grads, dbias, to_out, to_grads, to_bias, assign, rows, blocks, bias, s_in, s_out
):
    parts = 4
    some = U // parts

    def load(n):
        part = pl.ds(n * some, some)
        return pltpu.make_async_copy(grads.at[part], blocks.at[part], s_in.at[n])

    def store(d):
        return pltpu.make_async_copy(blocks.at[d], to_grads.at[assign[d]], s_out.at[d])

    ends = [(out, rows, to_out), (dbias, bias, to_bias)]
    first = [pltpu.make_async_copy(a, b, s_in.at[parts + n]) for n, (a, b, _) in enumerate(ends)]
    last = [pltpu.make_async_copy(b, c, s_out.at[U + n]) for n, (_, b, c) in enumerate(ends)]
    ids = pltpu.make_async_copy(users, assign, s_in.at[U])
    ids.start()
    for n in range(parts):
        load(n).start()
    for copy in first:
        copy.start()
    ids.wait()
    for n in range(parts):
        load(n).wait()
        for d in range(n * some, (n + 1) * some):
            store(d).start()
    for a, b in zip(first, last):
        a.wait()
        b.start()
    for d in range(U):
        store(d).wait()
    for copy in last:
        copy.wait()


def on_device(uvqk, lengths, assignment, buckets, rel_bias, cotangent):
    U = assignment.shape[0]
    H = rel_bias.shape[0]
    LEN = buckets.shape[0]
    D = H * W
    nt = LEN // TB
    tiles = nt * (nt + 1) // 2
    hbm = pl.BlockSpec(memory_space=pltpu.HBM)
    bf, f32 = jnp.bfloat16, jnp.float32
    dma = pltpu.SemaphoreType.DMA
    shapes = [
        jax.ShapeDtypeStruct((W, D), bf),
        jax.ShapeDtypeStruct((U, W, W), bf),
        jax.ShapeDtypeStruct((H, W), f32),
    ]

    out, grads, dbias = pl.pallas_call(
        functools.partial(kernel, H, U),
        out_shape=shapes,
        in_specs=[hbm] * 6,
        out_specs=[hbm, hbm, hbm],
        scratch_shapes=[
            pltpu.SMEM((U,), jnp.int32),
            pltpu.SMEM((U,), jnp.int32),
            pltpu.VMEM((U, W, W), bf),
            pltpu.VMEM((W, D), bf),
            pltpu.VMEM((1, LEN), jnp.int32),
            pltpu.VMEM((H, W), f32),
            pltpu.VMEM((H, W), f32),
            pltpu.VMEM((U, W, W), bf),
            pltpu.VMEM((4, LEN, W), bf),
            pltpu.VMEM((LEN, W), bf),
            pltpu.VMEM((LEN, W), bf),
            pltpu.VMEM((4, LEN, W), bf),
            pltpu.VMEM((nt, TB, TB), f32),
            pltpu.VMEM((tiles, TB, TB), bf),
            pltpu.VMEM((tiles, TB, TB), f32),
            pltpu.VMEM((nt, TB, TB), f32),
            pltpu.VMEM((W, LEN), bf),
            pltpu.VMEM((W, LEN), bf),
            pltpu.VMEM((W, LEN), f32),
            pltpu.VMEM((W, LEN), f32),
            pltpu.VMEM((W, LEN), bf),
            pltpu.VMEM((H, 4, H, W), f32),
            pltpu.VMEM((4, H, W), f32),
            pltpu.VMEM((1, 1, W), f32),
            pltpu.VMEM((U, 1, W), f32),
            pltpu.VMEM((1, 1, W), f32),
            pltpu.VMEM((1, 1, W), f32),
            pltpu.VMEM((H, 1, W), f32),
            dma((6,)),
            dma((U,)),
            dma((4 * H,)),
            dma((H,)),
            dma((H,)),
            dma((H,)),
            dma((H,)),
            dma((H,)),
            dma((H,)),
            dma((4 * H,)),
            dma((U,)),
            dma((U // H,)),
            dma((U,)),
            dma((H,)),
            dma,
            dma((H,)),
            dma((H,)),
        ],
        compiler_params=pltpu.CompilerParams(
            collective_id=0, has_side_effects=True, vmem_limit_bytes=60 * 1024 * 1024
        ),
        name="layer",
    )(
        assignment,
        lengths,
        uvqk,
        cotangent.reshape(W, D),
        buckets.reshape(1, LEN),
        rel_bias,
    )
    out, grads, dbias = pl.pallas_call(
        functools.partial(place, U),
        out_shape=shapes,
        in_specs=[hbm] * 4,
        out_specs=[hbm, hbm, hbm],
        scratch_shapes=[
            pltpu.SMEM((U,), jnp.int32),
            pltpu.VMEM((W, D), bf),
            pltpu.VMEM((U, W, W), bf),
            pltpu.VMEM((H, W), f32),
            dma((U + 2,)),
            dma((U + 2,)),
        ],
        compiler_params=pltpu.CompilerParams(vmem_limit_bytes=60 * 1024 * 1024),
        name="place",
    )(assignment, out, grads, dbias)
    return out.reshape(1, W, D), grads, dbias


def solution(mesh):
    in_specs = (P(None, "ctx", "dp"), P(), P(), P(), P(), P("dp", "ctx", None))
    out_specs = (P("dp", "ctx", None), P(None, "ctx", "dp"), P())
    return jax.shard_map(
        on_device, mesh=mesh, in_specs=in_specs, out_specs=out_specs, check_vma=False
    )
```

```python
import functools

import jax
import jax.numpy as jnp
from jax import lax
from jax.experimental import pallas as pl
from jax.experimental.pallas import tpu as pltpu
from jax.sharding import PartitionSpec as P

MESH = pl.DeviceIdType.MESH
Y = 4
TB = 512
W = 128
NN = (((1,), (0,)), ((), ()))
NT = (((1,), (1,)), ((), ()))


def mm(a, b, dims):
    return lax.dot_general(a, b, dims, preferred_element_type=jnp.float32)


def tile_at(ib, jb):
    return ib * (ib + 1) // 2 + jb


def ctx_of(h, p, H):
    if H != 8:
        return h
    y, b = lax.rem(h, 4), lax.div(h, 4)
    return lax.rem(y + 2 * b + lax.rem(p, 4), 4) * 2 + b


def head_of(c, p, H):
    if H != 8:
        return c
    x, b = lax.div(c, 2), lax.rem(c, 2)
    return b * 4 + lax.rem(x + 8 - 2 * b - lax.rem(p, 4), 4)


def kernel(
    H,
    U,
    assign_hbm,
    lengths_hbm,
    uvqk_hbm,
    cot_hbm,
    buckets_hbm,
    rel_hbm,
    out,
    grads,
    dbias_hbm,
    assign,
    lengths,
    uvqk,
    cot,
    buckets,
    rel,
    dbias,
    in_send,
    in_recv,
    cot_recv,
    out_send,
    g_send,
    toep,
    wts,
    dsl,
    diag,
    vt,
    kt,
    gt,
    at,
    dat,
    st_recv,
    st_send,
    db_send,
    db_recv,
    db_sum,
    db_mine,
    db_all,
    s_load,
    s_in,
    r_in,
    s_cot,
    r_cot,
    s_st,
    r_st,
    s_out,
    r_out,
    s_g,
    r_g,
    s_db,
    r_db,
    s_dbs,
    r_dbs,
    s_dba,
    r_dba,
):
    k = lax.axis_index("dp")
    c = lax.axis_index("ctx")
    e = lax.rem(k, H)
    comp = lax.div(k, H)
    head = head_of(c, k, H)
    own = e == head
    LEN = H * W
    nt = LEN // TB
    per = TB // W

    def rows(cc):
        if isinstance(cc, int):
            return pl.ds(cc * W, W)
        return pl.ds(pl.multiple_of(cc * W, W), W)

    def remote(src, dst, ss, rs, dev):
        return pltpu.make_async_remote_copy(
            src_ref=src, dst_ref=dst, send_sem=ss, recv_sem=rs, device_id=dev, device_id_type=MESH
        )

    def arrived(ref, ss, rs):
        remote(ref, ref, ss, rs, (k, c)).wait_recv()

    def loop(lo, hi, body):
        def step(i, _):
            body(i)
            return 0

        lax.fori_loop(lo, hi, step, 0)

    loads = [
        pltpu.make_async_copy(src, dst, s_load.at[n])
        for n, (src, dst) in enumerate(
            (
                (assign_hbm, assign),
                (uvqk_hbm, uvqk),
                (cot_hbm, cot),
                (lengths_hbm, lengths),
                (buckets_hbm, buckets),
                (rel_hbm, rel),
            )
        )
    ]
    for load in loads:
        load.start()
    barrier = pltpu.get_barrier_semaphore()

    for o in range(4 * H):
        far = (2, 3, 1, 0)[o // H]
        kk, cc = lax.rem(comp + far, 4) * H + head, lax.rem(c + o, H)
        if o % H or far:
            pl.semaphore_signal(barrier, inc=1, device_id=(kk, cc), device_id_type=MESH)
            continue

        @pl.when(kk != k)
        def _(kk=kk, cc=cc):
            pl.semaphore_signal(barrier, inc=1, device_id=(kk, cc), device_id_type=MESH)

    for o in range(1, H):
        pl.semaphore_signal(
            barrier, inc=1, device_id=(k, lax.rem(c + o, H)), device_id_type=MESH
        )

    for load in loads:
        load.wait()

    def arrange(p):
        in_send[p] = uvqk[assign[p]]

    loop(0, U, arrange)
    pl.semaphore_wait(barrier, U + H - 1 - own.astype(jnp.int32))

    z, y = lax.div(k, Y), lax.rem(k, Y)
    Z = U // Y

    def in_copy(o):
        dz, dy = (o // Y, o % Y) if isinstance(o, int) else (lax.div(o, Y), lax.rem(o, Y))
        p = lax.rem(z + dz, Z) * Y + lax.rem(y + dy, Y)
        return remote(
            in_send.at[p],
            in_recv.at[comp, rows(c)],
            s_in.at[o],
            r_in.at[comp * H + c],
            (p, ctx_of(e, p, H)),
        )

    @pl.when(jnp.logical_not(own))
    def _():
        in_copy(0).start()

    @pl.when(own)
    def _():
        pltpu.make_async_copy(
            in_send.at[k], in_recv.at[comp, rows(c)], r_in.at[comp * H + c]
        ).start()

    def cot_copy(o):
        cc = lax.rem(c + o, H)
        return remote(
            cot.at[:, rows(head_of(cc, k, H))],
            cot_recv.at[rows(c)],
            s_cot.at[o],
            r_cot.at[c],
            (k, cc),
        )

    ways = range(Z)
    turn = [dz * Y + dy for dz in ways for dy in range(Y)]
    for n, o in enumerate(turn):
        if o > 0:
            in_copy(o).start()
        if n % Y == 1 and 0 < n // Y + 1 < H:
            cot_copy(n // Y + 1).start()
    for o in range(len(ways) + 1, H):
        cot_copy(o).start()
    cot_recv[rows(c), :] = cot[:, rows(head)]

    eye = lax.broadcasted_iota(jnp.int32, (W, W), 0) == lax.broadcasted_iota(
        jnp.int32, (W, W), 1
    )
    onehot = lax.broadcasted_iota(jnp.int32, (W, LEN), 0) == buckets[...]
    rel_col = jnp.sum(jnp.where(eye, rel[pl.ds(head, 1), :], 0.0), axis=1, keepdims=True)
    relative = jnp.sum(jnp.where(onehot, rel_col, 0.0), axis=0, keepdims=True)
    row8 = lax.broadcasted_iota(jnp.int32, (8, 2 * TB), 0)
    for m in range(nt):
        low = relative[:, m * TB : (m + 1) * TB]
        before = relative[:, (m - 1) * TB : m * TB] if m else low
        x = jnp.broadcast_to(jnp.concatenate([low, before], 1), (8, 2 * TB))
        for bit in (1, 2, 4):
            x = jnp.where((row8 & bit) != 0, pltpu.roll(x, bit, 1), x)
        size = 8
        while size < TB:
            x = jnp.concatenate([x, pltpu.roll(x, size, 1)], 0)
            size *= 2
        toep[m] = x[:, :TB]

    def come(which, cc):
        arrived(in_recv.at[which, rows(cc)], s_in.at[0], r_in.at[which * H + cc])

    def turned(which, cc):
        block = in_recv[which, cc * W : (cc + 1) * W].astype(jnp.float32)
        return block.T.astype(jnp.bfloat16)

    user_len = lengths[assign[k]]
    for which in (1, 2, 3):
        for cc in range(H):
            come(which, cc)
    for cc in range(H):
        vt[:, cc * W : (cc + 1) * W] = turned(1, cc)
    key_at = lax.broadcasted_iota(jnp.int32, (TB, TB), 0)
    halves = min(2, nt)
    tiles, blocks = nt // halves, H // halves

    def forward(ib):
        query_at = lax.broadcasted_iota(jnp.int32, (1, TB), 1) + ib * TB
        limit = jnp.where(query_at < user_len, query_at, -1)
        q = in_recv[2, ib * TB : (ib + 1) * TB]
        acc = jnp.zeros((W, TB), jnp.float32)
        for jb in range(ib + 1):
            t = tile_at(ib, jb)
            score = mm(in_recv[3, jb * TB : (jb + 1) * TB], q, NT) + toep[ib - jb]
            live = key_at <= limit - jb * TB
            sig = 0.5 + 0.5 * jnp.tanh(0.5 * score)
            weight = score * sig
            slope = sig + weight * (1.0 - sig)
            wb = jnp.where(live, weight, 0.0).astype(jnp.bfloat16)
            wts[t] = wb
            dsl[t] = jnp.where(live, slope, 0.0)
            acc = acc + mm(vt[:, jb * TB : (jb + 1) * TB], wb, NN)
        at[:, ib * TB : (ib + 1) * TB] = acc

    def st_copy(half, o):
        cc = lax.rem(c + o, H)
        return remote(
            st_send.at[half],
            st_recv.at[half, c],
            s_st.at[half * H + o],
            r_st.at[half * H + c],
            (k, cc),
        )

    for half in range(halves):
        for ib in range(half * tiles, (half + 1) * tiles):
            forward(ib)
        means, spreads, gsums, gdots = [], [], [], []
        for cc in range(half * blocks, (half + 1) * blocks):
            blk = slice(cc * W, (cc + 1) * W)
            come(0, cc)

            @pl.when(c != cc)
            def _(cc=cc):
                arrived(cot_recv.at[rows(cc)], s_cot.at[0], r_cot.at[cc])

            grad = (cot_recv[blk].astype(jnp.float32) * in_recv[0, blk].astype(jnp.float32)).T
            gt[:, blk] = grad
            a = at[:, blk]
            mean = jnp.sum(a, axis=0, keepdims=True) * (1.0 / W)
            centered = a - mean
            means.append(mean)
            spreads.append(jnp.sum(centered * centered, axis=0, keepdims=True))
            gsums.append(jnp.sum(grad, axis=0, keepdims=True))
            gdots.append(jnp.sum(grad * centered, axis=0, keepdims=True))
        for n, rows_of in enumerate((means, spreads, gsums, gdots)):
            st_send[half, n] = jnp.concatenate(rows_of, 0)
        for o in range(1, H):
            st_copy(half, o).start()
        st_recv[half, c] = st_send[half]
    for cc in range(H):
        kt[:, cc * W : (cc + 1) * W] = turned(3, cc)

    D = H * W

    def normalise(half):
        def st_wait(o):
            cc = lax.rem(c + o, H)
            arrived(st_recv.at[half, cc], s_st.at[0], r_st.at[half * H + cc])

        loop(1, H, st_wait)
        mean = st_recv[half, 0, 0]
        for h in range(1, H):
            mean = mean + st_recv[half, h, 0]
        mean = mean * (1.0 / H)
        square = jnp.zeros_like(mean)
        g_total = jnp.zeros_like(mean)
        gn_total = jnp.zeros_like(mean)
        for h in range(H):
            off = st_recv[half, h, 0] - mean
            square = square + (st_recv[half, h, 1] + W * (off * off))
            g_total = g_total + st_recv[half, h, 2]
            gn_total = gn_total + (st_recv[half, h, 3] + off * st_recv[half, h, 2])
        inv = lax.rsqrt(square * (1.0 / D) + 1e-05)
        g_mean = g_total * (1.0 / D)
        gn_mean = gn_total * inv * (1.0 / D)
        for n in range(blocks):
            r = half * blocks + n
            blk = slice(r * W, (r + 1) * W)
            row = slice(n, n + 1)
            normed = (at[:, blk] - mean[row]) * inv[row]
            dat[:, blk] = (
                (gt[:, blk] - g_mean[row] - normed * gn_mean[row]) * inv[row]
            ).astype(jnp.bfloat16)
            natural = normed.T
            out_send[blk] = (natural * in_recv[0, blk].astype(jnp.float32)).astype(jnp.bfloat16)
            g_send[0, blk] = (natural * cot_recv[blk].astype(jnp.float32)).astype(jnp.bfloat16)

    def g_copy(which, o):
        cc = lax.rem(c + o, H)
        return remote(
            g_send.at[which, rows(cc)],
            grads.at[k],
            s_g.at[which * H + o],
            r_g.at[k],
            (which * H + head, cc),
        )

    early = range(1, min(3, blocks))

    def is_early(o):
        cc = lax.rem(c + o, H)
        turn_of = lax.rem(cc - c + H, blocks)
        return (cc < blocks) & (turn_of >= 1) & (turn_of < len(early) + 1)


    def g_start(o):
        for n in range(4):
            which = lax.rem(comp + n, 4)
            copy = g_copy(which, o)
            if o > 0:

                @pl.when(jnp.logical_not((which == 0) & is_early(o)))
                def _(copy=copy):
                    copy.start()

                continue
            mine = which * H + head == k

            @pl.when(jnp.logical_not(mine))
            def _(copy=copy):
                copy.start()

            @pl.when(mine)
            def _(which=which):
                pltpu.make_async_copy(g_send.at[which, rows(c)], grads.at[k], r_g.at[k]).start()

    def g_left(o):
        for which in range(4):
            if o > 0:
                g_copy(which, o).wait_send()
                continue

            @pl.when(which * H + head != k)
            def _(which=which):
                g_copy(which, 0).wait_send()

    def out_copy(o):
        cc = lax.rem(c + o, H)
        return remote(
            out_send.at[rows(cc)], out.at[:, rows(head)], s_out.at[o], r_out.at[c], (k, cc)
        )

    for half in range(halves):
        normalise(half)
        for n in range(blocks):
            cc = half * blocks + lax.rem(c + n, blocks)
            o = lax.rem(cc + H - c, H)
            if half == 0 and n in early:
                g_copy(0, o).start()

            @pl.when(o != 0)
            def _(o=o):
                out_copy(o).start()

    keep = pltpu.make_async_copy(out_send.at[rows(c)], out.at[:, rows(head)], s_out.at[0])
    keep.start()

    q_acc = [jnp.zeros((W, TB), jnp.float32) for _ in range(nt)]
    for jb in range(nt):
        value = in_recv[1, jb * TB : (jb + 1) * TB]
        acc = jnp.zeros((TB, W), jnp.float32)
        for ib in range(jb, nt):
            t = tile_at(ib, jb)
            ds = mm(value, dat[:, ib * TB : (ib + 1) * TB], NN) * dsl[t]
            if jb == 0:
                diag[ib - jb] = ds
            else:
                diag[ib - jb] += ds
            dsb = ds.astype(jnp.bfloat16)
            acc = acc + mm(dsb, in_recv[2, ib * TB : (ib + 1) * TB], NN)
            q_acc[ib] = q_acc[ib] + mm(kt[:, jb * TB : (jb + 1) * TB], dsb, NN)
        g_send[3, jb * TB : (jb + 1) * TB] = acc.astype(jnp.bfloat16)
    sheared = []
    for m in range(nt):
        x = jnp.concatenate([diag[m], jnp.zeros((TB, TB), jnp.float32)], 1)
        size = TB
        while size > 8:
            size //= 2
            x = x[:size] + pltpu.roll(x[size:], 2 * TB - size, 1)
        for bit in (1, 2, 4):
            x = jnp.where((row8 & bit) != 0, pltpu.roll(x, 2 * TB - bit, 1), x)
        sheared.append(jnp.sum(x, axis=0, keepdims=True))
    by_distance = []
    for m in range(nt):
        part = sheared[m][:, :TB]
        if m + 1 < nt:
            part = part + sheared[m + 1][:, TB:]
        by_distance.append(part)
    by_distance = jnp.concatenate(by_distance, 1)
    db_col = jnp.sum(jnp.where(onehot, by_distance, 0.0), axis=1, keepdims=True)
    db_send[0] = jnp.sum(jnp.where(eye, db_col, 0.0), axis=0, keepdims=True)

    collects = c == 0
    in_own = jnp.logical_and(collects, own)

    def db_copy(m):
        return remote(db_send.at[0], db_recv.at[k], s_db.at[m], r_db.at[k], (m * H + head, 0))

    def db_each(action):
        for m in range(U // H):

            @pl.when(jnp.logical_not(jnp.logical_and(m * H + head == k, collects)))
            def _(m=m):
                action(db_copy(m))

    db_each(lambda copy: copy.start())

    @pl.when(in_own)
    def _():
        db_recv[k] = db_send[0]

    for jb in range(nt):
        acc = jnp.zeros((TB, W), jnp.float32)
        for ib in range(jb, nt):
            acc = acc + mm(wts[tile_at(ib, jb)], dat[:, ib * TB : (ib + 1) * TB], NT)
        g_send[1, jb * TB : (jb + 1) * TB] = acc.astype(jnp.bfloat16)
    for ib in range(nt):
        for p in range(per):
            r = ib * per + p
            g_send[2, r * W : (r + 1) * W] = (
                q_acc[ib][:, p * W : (p + 1) * W].T.astype(jnp.bfloat16)
            )
    half, most = H // 2, H - max(1, H // 4)
    for o in range(half):
        g_start(o)
    for o in range(half // 2):
        g_left(o)

    def dbs_copy(j):
        p = comp * H + j
        return remote(db_sum.at[0], db_mine.at[0], s_dbs.at[j], r_dbs, (p, ctx_of(e, p, H)))

    @pl.when(collects)
    def _():
        def db_wait(o):
            p = lax.rem(k + o, U)

            @pl.when(jnp.logical_not(jnp.logical_and(o == 0, in_own)))
            def _():
                arrived(db_recv.at[p], s_db.at[0], r_db.at[p])

        loop(0, U, db_wait)
        db_sum[0] = jnp.sum(db_recv[...], axis=0)
        for j in range(H):

            @pl.when(jnp.logical_not(jnp.logical_and(in_own, comp * H + j == k)))
            def _(j=j):
                dbs_copy(j).start()

    for o in range(half, most):
        g_start(o)
    for o in range(half // 2, half):
        g_left(o)

    @pl.when(in_own)
    def _():
        db_mine[0] = db_sum[0]

    @pl.when(jnp.logical_not(in_own))
    def _():
        arrived(db_mine.at[0], s_dbs.at[0], r_dbs)

    def dba_copy(o):
        cc = lax.rem(c + o, H)
        return remote(db_mine.at[0], db_all.at[c], s_dba.at[o], r_dba.at[c], (k, cc))

    loop(1, H, lambda o: dba_copy(o).start())
    db_all[c] = db_mine[0]

    for o in range(most, H):
        g_start(o)

    def dba_wait(o):
        cc = lax.rem(c + o, H)
        arrived(db_all.at[cc], s_dba.at[0], r_dba.at[cc])

    loop(1, H, dba_wait)

    def dba_put(cc):
        dbias[pl.ds(head_of(cc, k, H), 1), :] = db_all[cc]

    loop(0, H, dba_put)
    put = pltpu.make_async_copy(dbias, dbias_hbm, s_load.at[0])
    put.start()

    keep.wait()
    put.wait()

    loop(0, U, lambda d: arrived(grads.at[d], s_g.at[0], r_g.at[d]))

    def ctx_end(o):
        cc = lax.rem(c + o, H)
        ref = out.at[:, rows(head_of(cc, k, H))]
        arrived(ref, s_out.at[0], r_out.at[cc])
        for half in range(halves):
            st_copy(half, o).wait_send()
        dba_copy(o).wait_send()
        cot_copy(o).wait_send()
        out_copy(o).wait_send()

    loop(1, H, ctx_end)

    @pl.when(jnp.logical_not(own))
    def _():
        in_copy(0).wait_send()

    loop(1, U, lambda o: in_copy(o).wait_send())
    for o in range(half, H):
        g_left(o)
    db_each(lambda copy: copy.wait_send())

    @pl.when(collects)
    def _():
        for j in range(H):

            @pl.when(jnp.logical_not(jnp.logical_and(in_own, comp * H + j == k)))
            def _(j=j):
                dbs_copy(j).wait_send()


def place(
    U, users, out, grads, dbias, to_out, to_grads, to_bias, assign, rows, blocks, bias, s_in, s_out
):
    parts = 4
    some = U // parts

    def load(n):
        part = pl.ds(n * some, some)
        return pltpu.make_async_copy(grads.at[part], blocks.at[part], s_in.at[n])

    def store(d):
        return pltpu.make_async_copy(blocks.at[d], to_grads.at[assign[d]], s_out.at[d])

    ends = [(out, rows, to_out), (dbias, bias, to_bias)]
    first = [pltpu.make_async_copy(a, b, s_in.at[parts + n]) for n, (a, b, _) in enumerate(ends)]
    last = [pltpu.make_async_copy(b, c, s_out.at[U + n]) for n, (_, b, c) in enumerate(ends)]
    ids = pltpu.make_async_copy(users, assign, s_in.at[U])
    ids.start()
    for n in range(parts):
        load(n).start()
    for copy in first:
        copy.start()
    ids.wait()
    for n in range(parts):
        load(n).wait()
        for d in range(n * some, (n + 1) * some):
            store(d).start()
    for a, b in zip(first, last):
        a.wait()
        b.start()
    for d in range(U):
        store(d).wait()
    for copy in last:
        copy.wait()


def on_device(uvqk, lengths, assignment, buckets, rel_bias, cotangent):
    U = assignment.shape[0]
    H = rel_bias.shape[0]
    LEN = buckets.shape[0]
    D = H * W
    nt = LEN // TB
    tiles = nt * (nt + 1) // 2
    halves = min(2, nt)
    hbm = pl.BlockSpec(memory_space=pltpu.HBM)
    bf, f32 = jnp.bfloat16, jnp.float32
    dma = pltpu.SemaphoreType.DMA
    shapes = [
        jax.ShapeDtypeStruct((W, D), bf),
        jax.ShapeDtypeStruct((U, W, W), bf),
        jax.ShapeDtypeStruct((H, W), f32),
    ]

    out, grads, dbias = pl.pallas_call(
        functools.partial(kernel, H, U),
        out_shape=shapes,
        in_specs=[hbm] * 6,
        out_specs=[hbm, hbm, hbm],
        scratch_shapes=[
            pltpu.SMEM((U,), jnp.int32),
            pltpu.SMEM((U,), jnp.int32),
            pltpu.VMEM((U, W, W), bf),
            pltpu.VMEM((W, D), bf),
            pltpu.VMEM((1, LEN), jnp.int32),
            pltpu.VMEM((H, W), f32),
            pltpu.VMEM((H, W), f32),
            pltpu.VMEM((U, W, W), bf),
            pltpu.VMEM((4, LEN, W), bf),
            pltpu.VMEM((LEN, W), bf),
            pltpu.VMEM((LEN, W), bf),
            pltpu.VMEM((4, LEN, W), bf),
            pltpu.VMEM((nt, TB, TB), f32),
            pltpu.VMEM((tiles, TB, TB), bf),
            pltpu.VMEM((tiles, TB, TB), f32),
            pltpu.VMEM((nt, TB, TB), f32),
            pltpu.VMEM((W, LEN), bf),
            pltpu.VMEM((W, LEN), bf),
            pltpu.VMEM((W, LEN), f32),
            pltpu.VMEM((W, LEN), f32),
            pltpu.VMEM((W, LEN), bf),
            pltpu.VMEM((halves, H, 4, H // halves, W), f32),
            pltpu.VMEM((halves, 4, H // halves, W), f32),
            pltpu.VMEM((1, 1, W), f32),
            pltpu.VMEM((U, 1, W), f32),
            pltpu.VMEM((1, 1, W), f32),
            pltpu.VMEM((1, 1, W), f32),
            pltpu.VMEM((H, 1, W), f32),
            dma((6,)),
            dma((U,)),
            dma((4 * H,)),
            dma((H,)),
            dma((H,)),
            dma((halves * H,)),
            dma((halves * H,)),
            dma((H,)),
            dma((H,)),
            dma((4 * H,)),
            dma((U,)),
            dma((U // H,)),
            dma((U,)),
            dma((H,)),
            dma,
            dma((H,)),
            dma((H,)),
        ],
        compiler_params=pltpu.CompilerParams(
            collective_id=0, has_side_effects=True, vmem_limit_bytes=60 * 1024 * 1024
        ),
        name="layer",
    )(
        assignment,
        lengths,
        uvqk,
        cotangent.reshape(W, D),
        buckets.reshape(1, LEN),
        rel_bias,
    )
    out, grads, dbias = pl.pallas_call(
        functools.partial(place, U),
        out_shape=shapes,
        in_specs=[hbm] * 4,
        out_specs=[hbm, hbm, hbm],
        scratch_shapes=[
            pltpu.SMEM((U,), jnp.int32),
            pltpu.VMEM((W, D), bf),
            pltpu.VMEM((U, W, W), bf),
            pltpu.VMEM((H, W), f32),
            dma((U + 2,)),
            dma((U + 2,)),
        ],
        compiler_params=pltpu.CompilerParams(vmem_limit_bytes=60 * 1024 * 1024),
        name="place",
    )(assignment, out, grads, dbias)
    return out.reshape(1, W, D), grads, dbias


def solution(mesh):
    in_specs = (P(None, "ctx", "dp"), P(), P(), P(), P(), P("dp", "ctx", None))
    out_specs = (P("dp", "ctx", None), P(None, "ctx", "dp"), P())
    return jax.shard_map(
        on_device, mesh=mesh, in_specs=in_specs, out_specs=out_specs, check_vma=False
    )
```
